512 devices in a mesh: tm: 32 (over z, core), space: 16 (over x, y).
Axes of the slice: x: 4, y: 4, z: 16, core: 2. Of those that a mesh axis runs over, the one named last changes fastest.
Arguments:
- snapshots: bfloat16 [16384, 4096], P('space', 'tm'), may hold values from -23 to 23
- energy: bfloat16 [128, 7, 128, 128], P('space'), may hold values from -0.375 to 0.375
- neighbours: int32 [128, 7], P('space'), may hold values from 0 to 127, as said below
- sketch: float32 [5, 256, 128], replicated, may hold values from -0.375 to 0.375
Outputs:
- modes: bfloat16 [6, 32, 16384, 128], P(None, 'tm', 'space')
The draws below stay inside these ranges and needn't reach their ends.
Inputs may be any that keep to these rules, and one draw needn't show every extreme that they name: `neighbours`: entry [b, k] lies within 2 blocks of b.
All inputs are finite; a program needn't handle non-finite values.
Results may differ from the reference program's by a relative error of at most 0.017.
Values may be sent and summed in bfloat16 or wider, within the bound.
A program may use at most 64 MiB of HBM per device.

```python
import math
import jax
import jax.numpy as jnp
from jax import lax

K = 128
BLK = 128
HB = 2
LEVELS = 5
NBLK = 128
ROWS = 16384
SNAPS = 4096
N_TM = 32


def draw_snapshots(key, part):
    key_scale, key_base = jax.random.split(key, 2)
    position = jnp.arange(ROWS, dtype=jnp.float32) / ROWS
    rising = 3.0 ** (0.5 * position)
    roughness = jnp.exp(jax.random.uniform(key_scale, (ROWS,), jnp.float32, 0.0, math.log(10.0))) / 4.6
    values = jnp.clip(jax.random.normal(key_base, (ROWS, SNAPS), jnp.float32), -6.0, 6.0)
    return ((rising * roughness)[:, None] * values).astype(jnp.bfloat16)


def draw_neighbours(key, part):
    raw_offsets = jax.random.randint(key, (NBLK, 7), 0, 2 * HB)
    offsets = jnp.where(raw_offsets < HB, raw_offsets - HB, raw_offsets - HB + 1)
    own_block = jnp.arange(NBLK, dtype=jnp.int32)[:, None]
    return jnp.clip(own_block + offsets, 0, NBLK - 1).astype(jnp.int32)


def block_levels(stream_key, shape, cuts, least, top_value):
    loudness, own = 1.0, jax.random.fold_in(stream_key, 6)
    for dim, parts in cuts:
        heights = jnp.exp(jax.random.uniform(jax.random.fold_in(own, dim), (parts,), jnp.float32, least / len(cuts), top_value / len(cuts)))
        loudness = loudness * jnp.repeat(heights, shape[dim] // parts).reshape([-1 if axis == dim else 1 for axis in range(len(shape))])
    return loudness


def scatter_about(stream_key, shape, deviation, bound, pieces=(), held_as=jnp.bfloat16):
    values = deviation * jax.random.normal(stream_key, shape, jnp.float32)
    if pieces:
        values = values * block_levels(stream_key, shape, pieces, -0.22, 0.18)
    return jnp.clip(values, -bound, bound).astype(held_as)


def setup_inputs(seed: int = 0) -> dict:
    streams_of = jax.random.split(jax.random.key(seed), 5)
    return {
        "snapshots": draw_snapshots(jax.random.fold_in(streams_of[4], 71), 0),
        "energy": scatter_about(streams_of[1], (NBLK, 7, BLK, BLK), (2 * BLK) ** -0.5, 0.375, ((0, 16),)),
        "neighbours": draw_neighbours(jax.random.fold_in(streams_of[4], 71), 0),
        "sketch": scatter_about(streams_of[3], (LEVELS, 2 * K, K), (2 * K) ** -0.5, 0.375, (), jnp.float32),
    }


def energy_apply(source, energy, neighbours):
    blocks = source.reshape(NBLK, BLK, source.shape[1])
    running = 3.0 * blocks.astype(jnp.float32)
    for slot_index in range(energy.shape[1]):
        gathered = jnp.take(blocks, neighbours[:, slot_index], axis=0).astype(jnp.float32)
        running = running + jnp.einsum('nij,njw->niw', energy[:, slot_index].astype(jnp.float32), gathered)
    return running.astype(jnp.bfloat16).reshape(ROWS, source.shape[1])

def orthonormal_leaf(window, energy, neighbours):
    energy_image = energy_apply(window, energy, neighbours)
    gram_matrix = jnp.dot(energy_image.T.astype(jnp.float32), energy_image.astype(jnp.float32), preferred_element_type=jnp.float32) / ROWS
    lower_factor = jnp.linalg.cholesky(gram_matrix)
    identity = jnp.eye(K, dtype=jnp.float32)
    coefficients = jax.scipy.linalg.solve_triangular(lower_factor, identity, lower=True).T.astype(jnp.bfloat16)
    level_modes = jnp.dot(window.astype(jnp.float32), coefficients.astype(jnp.float32), preferred_element_type=jnp.float32).astype(jnp.bfloat16)
    level_image = jnp.dot(energy_image.astype(jnp.float32), coefficients.astype(jnp.float32), preferred_element_type=jnp.float32).astype(jnp.bfloat16)
    return (level_modes, level_image)

def merge_pair(joined, joined_image, sketch_level):
    gram_matrix = jnp.dot(joined_image.T.astype(jnp.float32), joined_image.astype(jnp.float32), preferred_element_type=jnp.float32) / ROWS
    columns = jnp.dot(gram_matrix, sketch_level, precision=lax.Precision.HIGHEST)
    inner_gram = jnp.dot(columns.T, jnp.dot(gram_matrix, columns, precision=lax.Precision.HIGHEST), precision=lax.Precision.HIGHEST)
    lower_factor = jnp.linalg.cholesky(inner_gram)
    coefficients = jax.scipy.linalg.solve_triangular(lower_factor, columns.T, lower=True).T.astype(jnp.bfloat16)
    level_modes = jnp.dot(joined.astype(jnp.float32), coefficients.astype(jnp.float32), preferred_element_type=jnp.float32).astype(jnp.bfloat16)
    level_image = jnp.dot(joined_image.astype(jnp.float32), coefficients.astype(jnp.float32), preferred_element_type=jnp.float32).astype(jnp.bfloat16)
    return (level_modes, level_image)

def reference(snapshots, energy, neighbours, sketch):
    windows = snapshots.reshape(ROWS, N_TM, K).transpose(1, 0, 2)
    current, images = lax.map(lambda window: orthonormal_leaf(window, energy, neighbours), windows)
    levels_kept = [current]
    for tree_level in range(LEVELS):
        joined = jnp.concatenate([current[0::2], current[1::2]], axis=2)
        joined_image = jnp.concatenate([images[0::2], images[1::2]], axis=2)
        sketch_level = sketch[tree_level]
        current, images = lax.map(lambda pair_items: merge_pair(pair_items[0], pair_items[1], sketch_level), (joined, joined_image))
        levels_kept.append(jnp.repeat(current, 2 ** (tree_level + 1), axis=0))
    return jnp.stack(levels_kept)
```

```python
import functools

import jax
import jax.numpy as jnp
from jax import lax
from jax.experimental import pallas as pl
from jax.experimental.pallas import tpu as pltpu
from jax.sharding import PartitionSpec as P

K = 128
HB = 2
F32 = jnp.float32
BF16 = jnp.bfloat16
NN = ((1,), (0,))
NT = ((1,), (1,))
TN = ((0,), (0,))


def mm(a, b, dims=NN):
    return lax.dot_general(a, b, (dims, ((), ())), preferred_element_type=F32)


def split(a):
    high = a.astype(BF16)
    return high, (a - high.astype(F32)).astype(BF16)


def mm3(a, b, dims=NN):
    ah, al = split(a)
    bh, bl = split(b)
    return mm(ah, bh, dims) + (mm(ah, bl, dims) + mm(al, bh, dims))


def eliminate(t, n, nb):
    done = []
    for k0 in range(0, n, nb):
        rows = lax.broadcasted_iota(jnp.int32, t.shape, 0)
        cols = [jnp.broadcast_to(t[:, k0 + j : k0 + j + 1], t.shape) for j in range(nb)]
        for j in range(nb):
            pivot = 1.0 / cols[j][j : j + 1, :]
            factor = jnp.where(rows > j, cols[j] * pivot, 0.0)
            for i in range(j + 1, nb):
                cols[i] = cols[i] - factor * cols[i][j : j + 1, :]
            t = t - factor * t[j : j + 1, :]
        done.append(t[:nb])
        t = t[nb:]
    return jnp.concatenate(done, axis=0)


def factor_solve(a, rhs, nblk=64, nb=16):
    n = a.shape[0]
    rr = lax.broadcasted_iota(jnp.int32, (nblk, nblk), 0)
    cc = lax.broadcasted_iota(jnp.int32, (nblk, nblk), 1)
    eye = jnp.where(rr == cc, 1.0, 0.0).astype(F32)
    full = jnp.concatenate([a, rhs], axis=1)
    parts = []
    for p in range(0, n, nblk):
        t = eliminate(jnp.concatenate([full[:nblk, p : p + nblk], eye], axis=1), nblk, nb)
        d = jnp.sum(jnp.where(rr == cc, t[:, :nblk], 0.0), axis=1, keepdims=True)
        inverse = t[:, nblk:] * lax.rsqrt(d)
        top = mm3(inverse, full[:nblk])
        parts.append(top[:, n:])
        if p + nblk < n:
            lower = mm3(full[nblk:, p : p + nblk], inverse, NT)
            full = full[nblk:] - mm3(lower, top)
    return jnp.concatenate(parts, axis=0)


def kernel(ns, levels, nb_ref, snap, energy, sketch, out, pad, image, modes, joined_image, joined_modes, *scratch):
    (xp, rs_buf, tm_buf, ag_src, ag_buf, gram, halo_sem, rs_sem, tm_sem, ag_sem, im_sem, mo_sem, out_sem, loc_sem) = scratch
    rows = snap.shape[0]
    nblk = rows // K
    piece = K // ns
    scale = 1.0 / (rows * ns)
    t = lax.axis_index("tm")
    s = lax.axis_index("space")
    nt = 2**levels

    def peer(d):
        return lax.rem(s + d, ns)

    def member(level, d):
        size = 2**level
        return (t // size) * size + lax.rem(lax.rem(t, size) + d, size)

    barrier = pltpu.get_barrier_semaphore()

    def greet_space(d, c):
        pl.semaphore_signal(barrier, inc=1, device_id={"space": peer(d)}, device_id_type=pl.DeviceIdType.MESH)
        return c

    def greet_tm(d, c):
        pl.semaphore_signal(barrier, inc=1, device_id={"tm": lax.rem(t + d, nt)}, device_id_type=pl.DeviceIdType.MESH)
        return c

    lax.fori_loop(1, ns, greet_space, 0)
    lax.fori_loop(1, nt, greet_tm, 0)

    def remote(src, dst, send, recv, where):
        return pltpu.make_async_remote_copy(
            src_ref=src, dst_ref=dst, send_sem=send, recv_sem=recv, device_id=where,
            device_id_type=pl.DeviceIdType.MESH,
        )

    halo = HB * K
    pad[halo : halo + rows] = snap[...]
    first = s * nblk

    def image_block(b, source, base):
        last = source.shape[0] // K - 1
        places = [jnp.clip(nb_ref[b, k] - base, 0, last) for k in range(energy.shape[1])]
        blocks = [source[pl.ds(place * K, K), :] for place in places]
        left = jnp.concatenate([energy[b, k] for k in range(energy.shape[1])], axis=1)
        acc = 3.0 * snap[b * K : (b + 1) * K, :].astype(F32) + mm(left, jnp.concatenate(blocks, axis=0))
        image[0][b * K : (b + 1) * K, :] = acc.astype(BF16)

    for b in range(HB, nblk - HB):
        image_block(b, snap, first)

    pl.semaphore_wait(barrier, ns - 1 + nt - 1)

    up = remote(snap.at[0:halo], pad.at[halo + rows :], halo_sem.at[0], halo_sem.at[1], {"space": s - 1})
    down = remote(snap.at[rows - halo :], pad.at[0:halo], halo_sem.at[2], halo_sem.at[3], {"space": s + 1})

    @pl.when(s > 0)
    def _():
        up.start()

    @pl.when(s < ns - 1)
    def _():
        down.start()

    @pl.when(s == 0)
    def _():
        pad[0:halo] = jnp.zeros((halo, K), BF16)

    @pl.when(s == ns - 1)
    def _():
        pad[halo + rows :] = jnp.zeros((halo, K), BF16)

    @pl.when(s > 0)
    def _():
        down.wait_recv()

    @pl.when(s < ns - 1)
    def _():
        up.wait_recv()

    for b in (*range(HB), *range(nblk - HB, nblk)):
        image_block(b, pad, first - HB)

    def whole_sum(level, partial, shadow):
        xp[level] = partial

        def send_piece(d, c):
            q = peer(d)
            remote(
                xp.at[level, pl.ds(q * piece, piece)], rs_buf.at[level, ns - 1 - d],
                rs_sem.at[level, 0], rs_sem.at[level, 1], {"space": q},
            ).start()
            return c

        lax.fori_loop(1, ns, send_piece, 0)
        shadow()
        pltpu.make_async_copy(rs_buf.at[level], rs_buf.at[level], rs_sem.at[level, 1]).wait()
        total = xp[level, pl.ds(s * piece, piece), :]
        for i in range(ns - 1):
            total = total + rs_buf[level, i]
        size = 2**level
        if level:
            ag_src[level, 0] = total

            def send_member(d, c):
                remote(
                    ag_src.at[level, 0], tm_buf[level].at[size - 1 - d],
                    tm_sem.at[level, 0], tm_sem.at[level, 1], {"tm": member(level, d)},
                ).start()
                return c

            lax.fori_loop(1, size, send_member, 0)
            pltpu.make_async_copy(tm_buf[level], tm_buf[level], tm_sem.at[level, 1]).wait()
            for i in range(size - 1):
                total = total + tm_buf[level][i]
        total = total * scale
        ag_src[level, 1] = total

        def send_total(d, c):
            remote(
                ag_src.at[level, 1], ag_buf.at[level, ns - 1 - d],
                ag_sem.at[level, 0], ag_sem.at[level, 1], {"space": peer(d)},
            ).start()
            return c

        lax.fori_loop(1, ns, send_total, 0)
        gram[pl.ds(s * piece, piece), :] = total
        pltpu.make_async_copy(ag_buf.at[level], ag_buf.at[level], ag_sem.at[level, 1]).wait()
        for i in range(ns - 1):
            gram[pl.ds(peer(i + 1) * piece, piece), :] = ag_buf[level, i]
        return gram[...]

    def side_of(level):
        return lax.rem(t // 2 ** (level - 1), 2)

    def exchange(level, source, joined, sem):
        side = side_of(level)
        keep = rows // 2**level
        copy = remote(
            source[level - 1].at[pl.ds((1 - side) * keep, keep)], joined[level - 1].at[side],
            sem.at[level, 0], sem.at[level, 1], {"tm": t + (1 - 2 * side) * 2 ** (level - 1)},
        )
        copy.start()
        joined[level - 1][side] = source[level - 1][pl.ds(side * keep, keep), :]
        return copy

    sends = []
    offset = 0 * t

    def out_own(level, start):
        count = rows // 2**level
        copy = pltpu.make_async_copy(modes[level], out.at[level, 0, pl.ds(start, count)], loc_sem.at[level])
        copy.start()
        sends.append(copy.wait)

    def out_members(level, start):
        count = rows // 2**level
        size = 2**level

        def send_modes(d, c):
            remote(
                modes[level], out.at[level, 0, pl.ds(start, count)],
                out_sem.at[level, 0], out_sem.at[level, 1], {"tm": member(level, d)},
            ).start()
            return c

        lax.fori_loop(1, size, send_modes, 0)
        some = out.at[level, 0, 0 : rows - count]
        sends.append(pltpu.make_async_copy(some, some, out_sem.at[level, 0]).wait)
        sends.append(pltpu.make_async_copy(some, some, out_sem.at[level, 1]).wait)

    rr = lax.broadcasted_iota(jnp.int32, (K, K), 0)
    cc = lax.broadcasted_iota(jnp.int32, (K, K), 1)
    eye = jnp.where(rr == cc, 1.0, 0.0).astype(F32)
    first_gram = whole_sum(0, mm(image[0][...], image[0][...], TN), lambda: None)
    coef = factor_solve(first_gram, eye).astype(BF16)
    image[0][...] = mm(image[0][...], coef, NT).astype(BF16)
    image_copy = exchange(1, image, joined_image, im_sem)
    modes[0][...] = mm(snap[...], coef, NT).astype(BF16)
    modes_copy = exchange(1, modes, joined_modes, mo_sem)
    out_own(0, offset)

    for level in range(1, levels + 1):
        image_copy.wait_recv()
        sends.append(image_copy.wait_send)
        sends.append(modes_copy.wait_send)
        ji = joined_image[level - 1]
        jm = joined_modes[level - 1]
        st = sketch[level - 1]
        before = functools.partial(out_members, level - 1, offset) if level > 1 else (lambda: None)
        x = whole_sum(level, mm(ji[0], ji[1], TN), before)
        st0, st1 = st[:, :K], st[:, K:]
        y0 = st0 + mm3(st1, x, NT)
        y1 = st1 + mm3(st0, x)
        z0 = y0 + mm3(y1, x, NT)
        z1 = y1 + mm3(y0, x)
        y = jnp.concatenate([y0, y1], axis=1)
        z = jnp.concatenate([z0, z1], axis=1)
        coef = factor_solve(mm3(y, z, NT), y).astype(BF16)
        c0, c1 = coef[:, :K], coef[:, K:]
        offset = offset + side_of(level) * (rows // 2**level)
        if level < levels:
            image[level][...] = (mm(ji[0], c0, NT) + mm(ji[1], c1, NT)).astype(BF16)
            image_copy = exchange(level + 1, image, joined_image, im_sem)
        modes_copy.wait_recv()
        modes[level][...] = (mm(jm[0], c0, NT) + mm(jm[1], c1, NT)).astype(BF16)
        if level < levels:
            modes_copy = exchange(level + 1, modes, joined_modes, mo_sem)
        out_own(level, offset)
    out_members(levels, offset)

    @pl.when(s > 0)
    def _():
        up.wait_send()

    @pl.when(s < ns - 1)
    def _():
        down.wait_send()

    for level in range(levels + 1):
        pltpu.make_async_copy(rs_buf.at[level], rs_buf.at[level], rs_sem.at[level, 0]).wait()
        if level:
            pltpu.make_async_copy(tm_buf[level], tm_buf[level], tm_sem.at[level, 0]).wait()
        pltpu.make_async_copy(ag_buf.at[level], ag_buf.at[level], ag_sem.at[level, 0]).wait()
    for wait in sends:
        wait()


def on_device(ns, levels, snapshots, energy, neighbours, sketch):
    rows = snapshots.shape[0]
    count = levels + 1
    piece = K // ns
    chunk = lambda l: pltpu.VMEM((rows // 2**l, K), BF16)
    pair = lambda l: pltpu.VMEM((2, rows // 2**l, K), BF16)
    sems = lambda *shape: pltpu.SemaphoreType.DMA(shape)
    vmem = pl.BlockSpec(memory_space=pltpu.VMEM)
    return pl.pallas_call(
        functools.partial(kernel, ns, levels),
        out_shape=jax.ShapeDtypeStruct((count, 1, rows, K), BF16),
        in_specs=[pl.BlockSpec(memory_space=pltpu.SMEM), vmem, vmem, vmem],
        out_specs=pl.BlockSpec(memory_space=pl.ANY),
        scratch_shapes=[
            pltpu.VMEM((rows + 2 * HB * K, K), BF16),
            [chunk(l) for l in range(count)],
            [chunk(l) for l in range(count)],
            [pair(l) for l in range(1, count)],
            [pair(l) for l in range(1, count)],
            pltpu.VMEM((count, K, K), F32),
            pltpu.VMEM((count, ns - 1, piece, K), F32),
            [pltpu.VMEM((max(2**l - 1, 1), piece, K), F32) for l in range(count)],
            pltpu.VMEM((count, 2, piece, K), F32),
            pltpu.VMEM((count, ns - 1, piece, K), F32),
            pltpu.VMEM((K, K), F32),
            sems(4),
            sems(count, 2),
            sems(count, 2),
            sems(count, 2),
            sems(count, 2),
            sems(count, 2),
            sems(count, 2),
            sems(count),
        ],
        compiler_params=pltpu.CompilerParams(
            collective_id=0, has_side_effects=True, vmem_limit_bytes=40 * 1024 * 1024
        ),
    )(neighbours, snapshots, energy, jnp.swapaxes(sketch, 1, 2))


def solution(mesh):
    placed = (P("space", "tm"), P("space", None, None, None), P("space", None), P())
    ns = mesh.shape["space"]
    levels = mesh.shape["tm"].bit_length() - 1
    return jax.shard_map(
        functools.partial(on_device, ns, levels),
        mesh=mesh,
        in_specs=placed,
        out_specs=P(None, "tm", "space", None),
        check_vma=False,
    )
```

```python
import functools

import jax
import jax.numpy as jnp
from jax import lax
from jax.experimental import pallas as pl
from jax.experimental.pallas import tpu as pltpu
from jax.sharding import PartitionSpec as P

K = 128
HB = 2
F32 = jnp.float32
BF16 = jnp.bfloat16
NN = ((1,), (0,))
NT = ((1,), (1,))
TN = ((0,), (0,))


def mm(a, b, dims=NN):
    return lax.dot_general(a, b, (dims, ((), ())), preferred_element_type=F32)


def split(a):
    high = a.astype(BF16)
    return high, (a - high.astype(F32)).astype(BF16)


def mm3(a, b, dims=NN):
    ah, al = split(a)
    bh, bl = split(b)
    return mm(ah, bh, dims) + (mm(ah, bl, dims) + mm(al, bh, dims))


def eliminate(t, n, nb):
    done = []
    for k0 in range(0, n, nb):
        rows = lax.broadcasted_iota(jnp.int32, t.shape, 0)
        cols = [jnp.broadcast_to(t[:, k0 + j : k0 + j + 1], t.shape) for j in range(nb)]
        for j in range(nb):
            pivot = 1.0 / cols[j][j : j + 1, :]
            factor = jnp.where(rows > j, cols[j] * pivot, 0.0)
            for i in range(j + 1, nb):
                cols[i] = cols[i] - factor * cols[i][j : j + 1, :]
            t = t - factor * t[j : j + 1, :]
        done.append(t[:nb])
        t = t[nb:]
    return jnp.concatenate(done, axis=0)


def factor_solve(a, rhs, nblk=64, nb=16):
    n = a.shape[0]
    rr = lax.broadcasted_iota(jnp.int32, (nblk, nblk), 0)
    cc = lax.broadcasted_iota(jnp.int32, (nblk, nblk), 1)
    eye = jnp.where(rr == cc, 1.0, 0.0).astype(F32)
    full = jnp.concatenate([a, rhs], axis=1)
    parts = []
    for p in range(0, n, nblk):
        t = eliminate(jnp.concatenate([full[:nblk, p : p + nblk], eye], axis=1), nblk, nb)
        d = jnp.sum(jnp.where(rr == cc, t[:, :nblk], 0.0), axis=1, keepdims=True)
        inverse = t[:, nblk:] * lax.rsqrt(d)
        top = mm3(inverse, full[:nblk])
        parts.append(top[:, n:])
        if p + nblk < n:
            lower = mm3(full[nblk:, p : p + nblk], inverse, NT)
            full = full[nblk:] - mm3(lower, top)
    return jnp.concatenate(parts, axis=0)


def kernel(ns, levels, nb_ref, snap_hbm, energy_hbm, sketch_hbm, out, snap, energy, sketch, sketch_t, pad, *scratch):
    (image, gathered, last_modes, joined_image, joined_modes, xp, rs_buf, tm_buf, ag_src, ag_buf, gram) = scratch[:11]
    (in_sem, halo_sem, rs_sem, tm_sem, ag_sem, im_sem, mo_sem, ga_sem, sib_sem, out_sem) = scratch[11:]
    rows = snap.shape[0]
    half = rows // 2
    nblk = rows // K
    piece = K // ns
    scale = 1.0 / (rows * ns)
    t = lax.axis_index("tm")
    s = lax.axis_index("space")
    nt = 2**levels
    core = lax.rem(t, 2)
    halo = HB * K
    pads = pltpu.make_async_copy(snap_hbm, pad.at[pl.ds(halo, rows)], in_sem.at[0])
    loads = [
        pltpu.make_async_copy(snap_hbm, snap, in_sem.at[1]),
        pltpu.make_async_copy(energy_hbm, energy, in_sem.at[2]),
        pltpu.make_async_copy(sketch_hbm, sketch, in_sem.at[3]),
    ]

    def peer(d):
        return lax.rem(s + d, ns)

    def member(level, d):
        size = 2**level
        return (t // size) * size + lax.rem(lax.rem(t, size) + d, size)

    barrier = pltpu.get_barrier_semaphore()

    def greet_space(d, c):
        pl.semaphore_signal(barrier, inc=1, device_id={"space": peer(d)}, device_id_type=pl.DeviceIdType.MESH)
        return c

    def greet_tm(d, c):
        pl.semaphore_signal(barrier, inc=1, device_id={"tm": lax.rem(t + d, nt)}, device_id_type=pl.DeviceIdType.MESH)
        return c

    lax.fori_loop(1, nt, greet_tm, 0)
    lax.fori_loop(1, ns, greet_space, 0)
    for load in loads:
        load.start()
    pads.start()

    def remote(src, dst, send, recv, where):
        return pltpu.make_async_remote_copy(
            src_ref=src, dst_ref=dst, send_sem=send, recv_sem=recv, device_id=where,
            device_id_type=pl.DeviceIdType.MESH,
        )

    first = s * nblk

    def image_block(b, source, base):
        last = source.shape[0] // K - 1
        places = [jnp.clip(nb_ref[b, k] - base, 0, last) for k in range(energy.shape[1])]
        blocks = [source[pl.ds(place * K, K), :] for place in places]
        left = jnp.concatenate([energy[b, k] for k in range(energy.shape[1])], axis=1)
        acc = 3.0 * snap[b * K : (b + 1) * K, :].astype(F32) + mm(left, jnp.concatenate(blocks, axis=0))
        image[0][b * K : (b + 1) * K, :] = acc.astype(BF16)

    for load in loads:
        load.wait()
    for b in range(HB, nblk - HB):
        image_block(b, snap, first)
    for l in range(levels):
        sketch_t[l] = sketch[l].T
    pads.wait()

    pl.semaphore_wait(barrier, ns - 1 + nt - 1)

    up = remote(snap.at[0:halo], pad.at[halo + rows :], halo_sem.at[0], halo_sem.at[1], {"space": s - 1})
    down = remote(snap.at[rows - halo :], pad.at[0:halo], halo_sem.at[2], halo_sem.at[3], {"space": s + 1})

    @pl.when(s > 0)
    def _():
        up.start()

    @pl.when(s < ns - 1)
    def _():
        down.start()

    @pl.when(s == 0)
    def _():
        pad[0:halo] = jnp.zeros((halo, K), BF16)

    @pl.when(s == ns - 1)
    def _():
        pad[halo + rows :] = jnp.zeros((halo, K), BF16)

    @pl.when(s > 0)
    def _():
        down.wait_recv()

    @pl.when(s < ns - 1)
    def _():
        up.wait_recv()

    for b in (*range(HB), *range(nblk - HB, nblk)):
        image_block(b, pad, first - HB)

    def whole_sum(level, partial, shadow):
        xp[level] = partial

        def send_piece(d, c):
            q = peer(d)
            remote(
                xp.at[level, pl.ds(q * piece, piece)], rs_buf.at[level, ns - 1 - d],
                rs_sem.at[level, 0], rs_sem.at[level, 1], {"space": q},
            ).start()
            return c

        lax.fori_loop(1, ns, send_piece, 0)
        shadow()
        pltpu.make_async_copy(rs_buf.at[level], rs_buf.at[level], rs_sem.at[level, 1]).wait()
        total = xp[level, pl.ds(s * piece, piece), :]
        for i in range(ns - 1):
            total = total + rs_buf[level, i]
        size = 2**level
        if level:
            ag_src[level, 0] = total

            def send_member(d, c):
                remote(
                    ag_src.at[level, 0], tm_buf[level].at[size - 1 - d],
                    tm_sem.at[level, 0], tm_sem.at[level, 1], {"tm": member(level, d)},
                ).start()
                return c

            lax.fori_loop(1, size, send_member, 0)
            pltpu.make_async_copy(tm_buf[level], tm_buf[level], tm_sem.at[level, 1]).wait()
            for i in range(size - 1):
                total = total + tm_buf[level][i]
        total = total * scale
        ag_src[level, 1] = total

        def send_total(d, c):
            remote(
                ag_src.at[level, 1], ag_buf.at[level, ns - 1 - d],
                ag_sem.at[level, 0], ag_sem.at[level, 1], {"space": peer(d)},
            ).start()
            return c

        lax.fori_loop(1, ns, send_total, 0)
        gram[pl.ds(s * piece, piece), :] = total
        pltpu.make_async_copy(ag_buf.at[level], ag_buf.at[level], ag_sem.at[level, 1]).wait()
        for i in range(ns - 1):
            gram[pl.ds(peer(i + 1) * piece, piece), :] = ag_buf[level, i]
        return gram[...]

    def side_of(level):
        return lax.rem(t // 2 ** (level - 1), 2)

    sends = []

    def exchange(level, source, start, joined, sem):
        side = side_of(level)
        keep = rows // 2**level
        copy = remote(
            source.at[pl.ds(start + (1 - side) * keep, keep)], joined.at[side],
            sem.at[level, 0], sem.at[level, 1], {"tm": t + (1 - 2 * side) * 2 ** (level - 1)},
        )
        copy.start()
        joined[side] = source[pl.ds(start + side * keep, keep), :]
        sends.append(copy.wait_send)
        return copy

    def slot_of(level):
        return side_of(levels) if level == levels - 1 else 0

    def gather(level, start):
        count = rows // 2**level
        both = level == levels - 1
        size = 2 ** (level + 1) if both else 2**level
        mine = gathered[level].at[slot_of(level), pl.ds(start, count)]

        def send_modes(d, c):
            remote(
                mine, mine, ga_sem.at[level, 0], ga_sem.at[level, 1],
                {"tm": (t // size) * size + lax.rem(lax.rem(t, size) + 2 * d, size)},
            ).start()
            return c

        lax.fori_loop(1, size // 2, send_modes, 0)

    def gather_bytes(level, i):
        count = rows // 2**level
        size = 2 ** (level + 1) if level == levels - 1 else 2**level
        some = gathered[level].at[0, 0 : (size // 2 - 1) * count]
        return pltpu.make_async_copy(some, some, ga_sem.at[level, i])

    def needs_gather(level):
        return level > 1 or level == levels - 1

    def to_sibling(level):
        if needs_gather(level):
            gather_bytes(level, 1).wait()
            sends.append(gather_bytes(level, 0).wait)
        mine = gathered[level].at[:, pl.ds(core * half, half)]
        copy = remote(mine, mine, sib_sem.at[level, 0], sib_sem.at[level, 1], {"tm": t + 1 - 2 * core})
        copy.start()
        sends.append(copy.wait_send)
        return copy

    def store(level):
        copy = pltpu.make_async_copy(gathered[level].at[slot_of(level)], out.at[level, 0], out_sem.at[level])
        copy.start()
        sends.append(copy.wait)

    rr = lax.broadcasted_iota(jnp.int32, (K, K), 0)
    cc = lax.broadcasted_iota(jnp.int32, (K, K), 1)
    eye = jnp.where(rr == cc, 1.0, 0.0).astype(F32)
    first_gram = whole_sum(0, mm(image[0][...], image[0][...], TN), lambda: None)
    coef = factor_solve(first_gram, eye).astype(BF16)
    image[0][...] = mm(image[0][...], coef, NT).astype(BF16)
    image_copy = exchange(1, image[0], 0, joined_image[0], im_sem)
    gathered[0][0] = mm(snap[...], coef, NT).astype(BF16)
    modes_copy = exchange(1, gathered[0].at[0], 0, joined_modes[0], mo_sem)
    store(0)

    offset = 0 * t
    siblings = {}
    for level in range(1, levels + 1):
        image_copy.wait_recv()
        ji = joined_image[level - 1]
        jm = joined_modes[level - 1]

        def shadow(level=level, start=offset):
            if level - 1 >= 1 and needs_gather(level - 1):
                gather(level - 1, start)
            if level - 2 >= 1:
                siblings[level - 2].wait_recv()
                store(level - 2)

        x = whole_sum(level, mm(ji[0], ji[1], TN), shadow)
        if level - 1 >= 1:
            siblings[level - 1] = to_sibling(level - 1)
        st = sketch_t[level - 1]
        st0, st1 = st[:, :K], st[:, K:]
        y0 = st0 + mm3(st1, x, NT)
        y1 = st1 + mm3(st0, x)
        z0 = y0 + mm3(y1, x, NT)
        z1 = y1 + mm3(y0, x)
        y = jnp.concatenate([y0, y1], axis=1)
        z = jnp.concatenate([z0, z1], axis=1)
        coef = factor_solve(mm3(y, z, NT), y).astype(BF16)
        c0, c1 = coef[:, :K], coef[:, K:]
        keep = rows // 2**level
        offset = offset + side_of(level) * keep
        if level < levels:
            image[level][...] = (mm(ji[0], c0, NT) + mm(ji[1], c1, NT)).astype(BF16)
            image_copy = exchange(level + 1, image[level], 0, joined_image[level], im_sem)
            modes_copy.wait_recv()
            target = gathered[level].at[slot_of(level)]
            target[pl.ds(offset, keep), :] = (mm(jm[0], c0, NT) + mm(jm[1], c1, NT)).astype(BF16)
            if level < levels - 1:
                modes_copy = exchange(level + 1, target, offset, joined_modes[level], mo_sem)
        else:
            siblings[level - 1].wait_recv()
            store(level - 1)
            pair = gathered[level - 1]
            for i in range(4):
                part = slice(i * rows // 4, (i + 1) * rows // 4)
                last_modes[part] = (mm(pair[0, part], c0, NT) + mm(pair[1, part], c1, NT)).astype(BF16)
                copy = pltpu.make_async_copy(last_modes.at[part], out.at[level, 0, part], out_sem.at[level + i])
                copy.start()
                sends.append(copy.wait)

    @pl.when(s > 0)
    def _():
        up.wait_send()

    @pl.when(s < ns - 1)
    def _():
        down.wait_send()

    for level in range(levels + 1):
        pltpu.make_async_copy(rs_buf.at[level], rs_buf.at[level], rs_sem.at[level, 0]).wait()
        if level:
            pltpu.make_async_copy(tm_buf[level], tm_buf[level], tm_sem.at[level, 0]).wait()
        pltpu.make_async_copy(ag_buf.at[level], ag_buf.at[level], ag_sem.at[level, 0]).wait()
    for wait in sends:
        wait()


def on_device(ns, levels, snapshots, energy, neighbours, sketch):
    rows = snapshots.shape[0]
    count = levels + 1
    piece = K // ns
    sems = lambda *shape: pltpu.SemaphoreType.DMA(shape)
    hbm = pl.BlockSpec(memory_space=pltpu.HBM)
    return pl.pallas_call(
        functools.partial(kernel, ns, levels),
        out_shape=jax.ShapeDtypeStruct((count, 1, rows, K), BF16),
        in_specs=[pl.BlockSpec(memory_space=pltpu.SMEM), hbm, hbm, hbm],
        out_specs=hbm,
        scratch_shapes=[
            pltpu.VMEM(snapshots.shape, BF16),
            pltpu.VMEM(energy.shape, BF16),
            pltpu.VMEM(sketch.shape, F32),
            pltpu.VMEM((levels, K, 2 * K), F32),
            pltpu.VMEM((rows + 2 * HB * K, K), BF16),
            [pltpu.VMEM((rows // 2**l, K), BF16) for l in range(levels)],
            [pltpu.VMEM((2 if l == levels - 1 else 1, rows, K), BF16) for l in range(levels)],
            pltpu.VMEM((rows, K), BF16),
            [pltpu.VMEM((2, rows // 2**l, K), BF16) for l in range(1, count)],
            [pltpu.VMEM((2, rows // 2**l, K), BF16) for l in range(1, count)],
            pltpu.VMEM((count, K, K), F32),
            pltpu.VMEM((count, ns - 1, piece, K), F32),
            [pltpu.VMEM((max(2**l - 1, 1), piece, K), F32) for l in range(count)],
            pltpu.VMEM((count, 2, piece, K), F32),
            pltpu.VMEM((count, ns - 1, piece, K), F32),
            pltpu.VMEM((K, K), F32),
            sems(4),
            sems(4),
            *[sems(count, 2)] * 7,
            sems(count + 4),
        ],
        compiler_params=pltpu.CompilerParams(
            collective_id=0, has_side_effects=True, vmem_limit_bytes=40 * 1024 * 1024
        ),
    )(neighbours, snapshots, energy, sketch)


def solution(mesh):
    placed = (P("space", "tm"), P("space", None, None, None), P("space", None), P())
    ns = mesh.shape["space"]
    levels = mesh.shape["tm"].bit_length() - 1
    return jax.shard_map(
        functools.partial(on_device, ns, levels),
        mesh=mesh,
        in_specs=placed,
        out_specs=P(None, "tm", "space", None),
        check_vma=False,
    )
```

```python
import functools

import jax
import jax.numpy as jnp
from jax import lax
from jax.experimental import pallas as pl
from jax.experimental.pallas import tpu as pltpu
from jax.sharding import PartitionSpec as P

K = 128
HB = 2
CAP = 3
F32 = jnp.float32
BF16 = jnp.bfloat16
NN = ((1,), (0,))
NT = ((1,), (1,))
TN = ((0,), (0,))


def mm(a, b, dims=NN):
    return lax.dot_general(a, b, (dims, ((), ())), preferred_element_type=F32)


def split(a):
    high = a.astype(BF16)
    return high, (a - high.astype(F32)).astype(BF16)


def mm3(a, b, dims=NN):
    ah, al = split(a)
    bh, bl = split(b)
    return mm(ah, bh, dims) + (mm(ah, bl, dims) + mm(al, bh, dims))


def mm2(a, b, dims=NN):
    ah, al = split(a)
    return mm(ah, b, dims) + mm(al, b, dims)


def eliminate(t, n, nb):
    done = []
    for k0 in range(0, n, nb):
        rows = lax.broadcasted_iota(jnp.int32, t.shape, 0)
        cols = [jnp.broadcast_to(t[:, k0 + j : k0 + j + 1], t.shape) for j in range(nb)]
        for j in range(nb):
            pivot = 1.0 / cols[j][j : j + 1, :]
            factor = jnp.where(rows > j, cols[j] * pivot, 0.0)
            for i in range(j + 1, nb):
                cols[i] = cols[i] - factor * cols[i][j : j + 1, :]
            t = t - factor * t[j : j + 1, :]
        done.append(t[:nb])
        t = t[nb:]
    return jnp.concatenate(done, axis=0)


def factor_solve(a, rhs, nblk=64, nb=16):
    n = a.shape[0]
    rr = lax.broadcasted_iota(jnp.int32, (nblk, nblk), 0)
    cc = lax.broadcasted_iota(jnp.int32, (nblk, nblk), 1)
    eye = jnp.where(rr == cc, 1.0, 0.0).astype(F32)
    full = jnp.concatenate([a, rhs], axis=1)
    parts = []
    for p in range(0, n, nblk):
        t = eliminate(jnp.concatenate([full[:nblk, p : p + nblk], eye], axis=1), nblk, nb)
        d = jnp.sum(jnp.where(rr == cc, t[:, :nblk], 0.0), axis=1, keepdims=True)
        inverse = t[:, nblk:] * lax.rsqrt(d)
        top = mm3(inverse, full[:nblk])
        parts.append(top[:, n:])
        if p + nblk < n:
            lower = mm3(full[nblk:, p : p + nblk], inverse, NT)
            full = full[nblk:] - mm3(lower, top)
    return jnp.concatenate(parts, axis=0)


def split_of(level):
    return min(level, CAP)


def kernel(ns, levels, nb_ref, snap_hbm, energy_hbm, sketch_hbm, out, snap, energy, sketch, sketch_t, pad, *scratch):
    (image, gathered, last_modes, joined_energy, joined_image, joined_modes, xp, rs_buf, tm_buf) = scratch[:9]
    (ag_src, ag_buf, gram, coefs) = scratch[9:13]
    (in_sem, halo_sem, rs_sem, tm_sem, ag_sem, im_sem, mo_sem, ga_sem, sib_sem, co_sem, out_sem) = scratch[13:]
    rows = snap.shape[0]
    half = rows // 2
    nblk = rows // K
    piece = K // ns
    scale = 1.0 / (rows * ns)
    t = lax.axis_index("tm")
    s = lax.axis_index("space")
    nt = 2**levels
    core = lax.rem(t, 2)
    halo = HB * K
    pads = pltpu.make_async_copy(snap_hbm, pad.at[pl.ds(halo, rows)], in_sem.at[0])
    loads = [
        pltpu.make_async_copy(snap_hbm, snap, in_sem.at[1]),
        pltpu.make_async_copy(energy_hbm, energy, in_sem.at[2]),
        pltpu.make_async_copy(sketch_hbm, sketch, in_sem.at[3]),
    ]

    def peer(d):
        return lax.rem(s + d, ns)

    def member(level, d):
        size = 2**level
        return (t // size) * size + lax.rem(lax.rem(t, size) + d, size)

    barrier = pltpu.get_barrier_semaphore()

    def greet_space(d, c):
        pl.semaphore_signal(barrier, inc=1, device_id={"space": peer(d)}, device_id_type=pl.DeviceIdType.MESH)
        return c

    def greet_tm(d, c):
        pl.semaphore_signal(barrier, inc=1, device_id={"tm": lax.rem(t + d, nt)}, device_id_type=pl.DeviceIdType.MESH)
        return c

    lax.fori_loop(1, nt, greet_tm, 0)
    lax.fori_loop(1, ns, greet_space, 0)
    for load in loads:
        load.start()
    pads.start()

    def remote(src, dst, send, recv, where):
        return pltpu.make_async_remote_copy(
            src_ref=src, dst_ref=dst, send_sem=send, recv_sem=recv, device_id=where,
            device_id_type=pl.DeviceIdType.MESH,
        )

    first = s * nblk

    def image_block(b, source, base):
        last = source.shape[0] // K - 1
        places = [jnp.clip(nb_ref[b, k] - base, 0, last) for k in range(energy.shape[1])]
        blocks = [source[pl.ds(place * K, K), :] for place in places]
        left = jnp.concatenate([energy[b, k] for k in range(energy.shape[1])], axis=1)
        acc = 3.0 * snap[b * K : (b + 1) * K, :].astype(F32) + mm(left, jnp.concatenate(blocks, axis=0))
        image[0][b * K : (b + 1) * K, :] = acc.astype(BF16)

    for load in loads:
        load.wait()
    for b in range(HB, nblk - HB):
        image_block(b, snap, first)
    for l in range(levels):
        sketch_t[l] = sketch[l].T
    pads.wait()

    pl.semaphore_wait(barrier, ns - 1 + nt - 1)

    up = remote(snap.at[0:halo], pad.at[halo + rows :], halo_sem.at[0], halo_sem.at[1], {"space": s - 1})
    down = remote(snap.at[rows - halo :], pad.at[0:halo], halo_sem.at[2], halo_sem.at[3], {"space": s + 1})

    @pl.when(s > 0)
    def _():
        up.start()

    @pl.when(s < ns - 1)
    def _():
        down.start()

    @pl.when(s == 0)
    def _():
        pad[0:halo] = jnp.zeros((halo, K), BF16)

    @pl.when(s == ns - 1)
    def _():
        pad[halo + rows :] = jnp.zeros((halo, K), BF16)

    @pl.when(s > 0)
    def _():
        down.wait_recv()

    @pl.when(s < ns - 1)
    def _():
        up.wait_recv()

    for b in (*range(HB), *range(nblk - HB, nblk)):
        image_block(b, pad, first - HB)

    def sum_start(level, partial):
        xp[level] = partial

        def send_piece(d, c):
            q = peer(d)
            remote(
                xp.at[level, pl.ds(q * piece, piece)], rs_buf.at[level, ns - 1 - d],
                rs_sem.at[level, 0], rs_sem.at[level, 1], {"space": q},
            ).start()
            return c

        lax.fori_loop(1, ns, send_piece, 0)

    def sum_members(level):
        pltpu.make_async_copy(rs_buf.at[level], rs_buf.at[level], rs_sem.at[level, 1]).wait()
        total = xp[level, pl.ds(s * piece, piece), :]
        for i in range(ns - 1):
            total = total + rs_buf[level, i]
        size = 2 ** split_of(level)
        ag_src[level, 0] = total

        def send_member(d, c):
            remote(
                ag_src.at[level, 0], tm_buf[level].at[size - 1 - d],
                tm_sem.at[level, 0], tm_sem.at[level, 1], {"tm": member(split_of(level), d)},
            ).start()
            return c

        lax.fori_loop(1, size, send_member, 0)

    def sum_back(level):
        size = 2 ** split_of(level)
        total = ag_src[level, 0]
        if level:
            pltpu.make_async_copy(tm_buf[level], tm_buf[level], tm_sem.at[level, 1]).wait()
            for i in range(size - 1):
                total = total + tm_buf[level][i]
        total = total * scale
        ag_src[level, 1] = total

        def send_total(d, c):
            remote(
                ag_src.at[level, 1], ag_buf.at[level, ns - 1 - d],
                ag_sem.at[level, 0], ag_sem.at[level, 1], {"space": peer(d)},
            ).start()
            return c

        lax.fori_loop(1, ns, send_total, 0)

    def sum_end(level):
        gram[pl.ds(s * piece, piece), :] = ag_src[level, 1]
        pltpu.make_async_copy(ag_buf.at[level], ag_buf.at[level], ag_sem.at[level, 1]).wait()
        for i in range(ns - 1):
            gram[pl.ds(peer(i + 1) * piece, piece), :] = ag_buf[level, i]
        return gram[...]

    def side_of(level):
        return lax.rem(t // 2 ** (level - 1), 2)

    sends = []

    def exchange(level, source, start, joined, sem):
        side = side_of(level)
        keep = rows // 2 ** split_of(level)
        other, own = ((1 - side) * keep, side * keep) if level <= CAP else (0, 0)
        copy = remote(
            source.at[pl.ds(start + other, keep)], joined.at[side],
            sem.at[level, 0], sem.at[level, 1], {"tm": t + (1 - 2 * side) * 2 ** (level - 1)},
        )
        copy.start()
        joined[side] = source[pl.ds(start + own, keep), :]
        sends.append(copy.wait_send)
        return copy

    def slot_of(level):
        return side_of(levels) if level == levels - 1 else 0

    def mine(level, start):
        return gathered[level].at[:, pl.ds(start, rows // 2 ** split_of(level))]

    def gather(level, start):
        size = 2 ** split_of(level)

        def send_modes(d, c):
            remote(
                mine(level, start), mine(level, start), ga_sem.at[level, 0], ga_sem.at[level, 1],
                {"tm": member(split_of(level), 2 * d)},
            ).start()
            return c

        lax.fori_loop(1, size // 2, send_modes, 0)

    def gather_bytes(level, i):
        count = rows // 2 ** split_of(level)
        some = gathered[level].at[:, 0 : (2 ** split_of(level) // 2 - 1) * count]
        return pltpu.make_async_copy(some, some, ga_sem.at[level, i])

    def to_sibling(level):
        if split_of(level) > 1:
            gather_bytes(level, 1).wait()
            sends.append(gather_bytes(level, 0).wait)
        whole = gathered[level].at[:, pl.ds(core * half, half)]
        copy = remote(whole, whole, sib_sem.at[level, 0], sib_sem.at[level, 1], {"tm": t + 1 - 2 * core})
        copy.start()
        sends.append(copy.wait_send)
        return copy

    def store(level):
        copy = pltpu.make_async_copy(gathered[level].at[slot_of(level)], out.at[level, 0], out_sem.at[level])
        copy.start()
        sends.append(copy.wait)

    rr = lax.broadcasted_iota(jnp.int32, (K, K), 0)
    cc = lax.broadcasted_iota(jnp.int32, (K, K), 1)
    eye = jnp.where(rr == cc, 1.0, 0.0).astype(F32)
    energy_copy = exchange(1, image[0], 0, joined_energy, im_sem)
    sum_start(0, mm(image[0][...], image[0][...], TN))
    energy_copy.wait_recv()
    sum_start(1, mm(joined_energy[0], joined_energy[1], TN))
    sum_members(0)
    sum_back(0)
    sum_members(1)
    sum_back(1)
    coef = factor_solve(sum_end(0), eye).astype(BF16)
    coefs[core] = coef
    coefs_copy = remote(coefs.at[core], coefs.at[core], co_sem.at[0], co_sem.at[1], {"tm": t + 1 - 2 * core})
    coefs_copy.start()
    sends.append(coefs_copy.wait_send)
    gathered[0][0] = mm(snap[...], coef, NT).astype(BF16)
    modes_copy = exchange(1, gathered[0].at[0], 0, joined_modes[0], mo_sem)
    store(0)

    offset = 0 * t
    siblings = {}
    for level in range(1, levels + 1):
        ji = joined_image[level - 1]
        jm = joined_modes[level - 1]
        if level == 1:
            coefs_copy.wait_recv()
            for i in range(2):
                ji[i] = mm(joined_energy[i], coefs[i], NT).astype(BF16)
            x = mm2(mm2(sum_end(1), coefs[1], NT).T, coefs[0], NT).T
        else:
            image_copy.wait_recv()
            sum_start(level, mm(ji[0], ji[1], TN))
            if level - 1 >= 1 and level < levels and split_of(level - 1) > 1:
                gather(level - 1, offset)
            if level - 2 >= 1:
                siblings[level - 2].wait_recv()
                store(level - 2)
            sum_members(level)
            if level == levels:
                modes_copy.wait_recv()
                if split_of(level - 1) > 1:
                    gather(level - 1, offset)
            sum_back(level)
            x = sum_end(level)
            siblings[level - 1] = to_sibling(level - 1)
        st = sketch_t[level - 1]
        st0, st1 = st[:, :K], st[:, K:]
        y0 = st0 + mm3(st1, x, NT)
        y1 = st1 + mm3(st0, x)
        z0 = y0 + mm3(y1, x, NT)
        z1 = y1 + mm3(y0, x)
        y = jnp.concatenate([y0, y1], axis=1)
        z = jnp.concatenate([z0, z1], axis=1)
        coef = factor_solve(mm3(y, z, NT), y).astype(BF16)
        c0, c1 = coef[:, :K], coef[:, K:]
        keep = rows // 2 ** split_of(level)
        if level <= CAP:
            offset = offset + side_of(level) * keep
        if level < levels:
            image[level][...] = (mm(ji[0], c0, NT) + mm(ji[1], c1, NT)).astype(BF16)
            image_copy = exchange(level + 1, image[level], 0, joined_image[level], im_sem)
            modes_copy.wait_recv()
            target = gathered[level].at[slot_of(level)]
            target[pl.ds(offset, keep), :] = (mm(jm[0], c0, NT) + mm(jm[1], c1, NT)).astype(BF16)
            if level < levels - 1:
                modes_copy = exchange(level + 1, target, offset, joined_modes[level], mo_sem)
            else:
                side = side_of(levels)
                chunk = target.at[pl.ds(offset, keep)]
                modes_copy = remote(
                    chunk, chunk, mo_sem.at[levels, 0], mo_sem.at[levels, 1],
                    {"tm": t + (1 - 2 * side) * 2 ** (levels - 1)},
                )
                modes_copy.start()
                sends.append(modes_copy.wait_send)
        else:
            siblings[level - 1].wait_recv()
            store(level - 1)
            pair = gathered[level - 1]
            for i in range(4):
                part = slice(i * rows // 4, (i + 1) * rows // 4)
                last_modes[part] = (mm(pair[0, part], c0, NT) + mm(pair[1, part], c1, NT)).astype(BF16)
                copy = pltpu.make_async_copy(last_modes.at[part], out.at[level, 0, part], out_sem.at[level + i])
                copy.start()
                sends.append(copy.wait)

    @pl.when(s > 0)
    def _():
        up.wait_send()

    @pl.when(s < ns - 1)
    def _():
        down.wait_send()

    for level in range(levels + 1):
        pltpu.make_async_copy(rs_buf.at[level], rs_buf.at[level], rs_sem.at[level, 0]).wait()
        if level:
            pltpu.make_async_copy(tm_buf[level], tm_buf[level], tm_sem.at[level, 0]).wait()
        pltpu.make_async_copy(ag_buf.at[level], ag_buf.at[level], ag_sem.at[level, 0]).wait()
    for wait in sends:
        wait()


def on_device(ns, levels, snapshots, energy, neighbours, sketch):
    rows = snapshots.shape[0]
    half = rows // 2
    count = levels + 1
    piece = K // ns
    sems = lambda *shape: pltpu.SemaphoreType.DMA(shape)
    hbm = pl.BlockSpec(memory_space=pltpu.HBM)
    return pl.pallas_call(
        functools.partial(kernel, ns, levels),
        out_shape=jax.ShapeDtypeStruct((count, 1, rows, K), BF16),
        in_specs=[pl.BlockSpec(memory_space=pltpu.SMEM), hbm, hbm, hbm],
        out_specs=hbm,
        scratch_shapes=[
            pltpu.VMEM(snapshots.shape, BF16),
            pltpu.VMEM(energy.shape, BF16),
            pltpu.VMEM(sketch.shape, F32),
            pltpu.VMEM((levels, K, 2 * K), F32),
            pltpu.VMEM((rows + 2 * HB * K, K), BF16),
            [pltpu.VMEM((rows // 2 ** split_of(l), K), BF16) for l in range(levels)],
            [pltpu.VMEM((2 if l == levels - 1 else 1, rows, K), BF16) for l in range(levels)],
            pltpu.VMEM((rows, K), BF16),
            pltpu.VMEM((2, half, K), BF16),
            [pltpu.VMEM((2, rows // 2 ** split_of(l), K), BF16) for l in range(1, count)],
            [pltpu.VMEM((2, rows // 2 ** split_of(l), K), BF16) for l in range(1, count)],
            pltpu.VMEM((count, K, K), F32),
            pltpu.VMEM((count, ns - 1, piece, K), F32),
            [pltpu.VMEM((max(2 ** split_of(l) - 1, 1), piece, K), F32) for l in range(count)],
            pltpu.VMEM((count, 2, piece, K), F32),
            pltpu.VMEM((count, ns - 1, piece, K), F32),
            pltpu.VMEM((K, K), F32),
            pltpu.VMEM((2, K, K), BF16),
            sems(4),
            sems(4),
            *[sems(count, 2)] * 7,
            sems(2),
            sems(count + 4),
        ],
        compiler_params=pltpu.CompilerParams(
            collective_id=0, has_side_effects=True, vmem_limit_bytes=40 * 1024 * 1024
        ),
    )(neighbours, snapshots, energy, sketch)


def solution(mesh):
    placed = (P("space", "tm"), P("space", None, None, None), P("space", None), P())
    ns = mesh.shape["space"]
    levels = mesh.shape["tm"].bit_length() - 1
    return jax.shard_map(
        functools.partial(on_device, ns, levels),
        mesh=mesh,
        in_specs=placed,
        out_specs=P(None, "tm", "space", None),
        check_vma=False,
    )
```

```python
import functools

import jax
import jax.numpy as jnp
from jax import lax
from jax.experimental import pallas as pl
from jax.experimental.pallas import tpu as pltpu
from jax.sharding import PartitionSpec as P

K = 128
HB = 2
CAP = 3
AHEAD = 3
F32 = jnp.float32
BF16 = jnp.bfloat16
NN = ((1,), (0,))
NT = ((1,), (1,))
TN = ((0,), (0,))


def mm(a, b, dims=NN):
    return lax.dot_general(a, b, (dims, ((), ())), preferred_element_type=F32)


def split(a):
    high = a.astype(BF16)
    return high, (a - high.astype(F32)).astype(BF16)


def mm3(a, b, dims=NN):
    ah, al = split(a)
    bh, bl = split(b)
    return mm(ah, bh, dims) + (mm(ah, bl, dims) + mm(al, bh, dims))


def mm2(a, b, dims=NN):
    ah, al = split(a)
    return mm(ah, b, dims) + mm(al, b, dims)


def around(a, middle, b):
    high, low = split(mm2(middle, b, NT))
    return mm(a, high) + mm(a, low)


def eliminate(t, n, nb):
    done = []
    for k0 in range(0, n, nb):
        rows = lax.broadcasted_iota(jnp.int32, t.shape, 0)
        cols = [jnp.broadcast_to(t[:, k0 + j : k0 + j + 1], t.shape) for j in range(nb)]
        for j in range(nb):
            pivot = 1.0 / cols[j][j : j + 1, :]
            factor = jnp.where(rows > j, cols[j] * pivot, 0.0)
            for i in range(j + 1, nb):
                cols[i] = cols[i] - factor * cols[i][j : j + 1, :]
            t = t - factor * t[j : j + 1, :]
        done.append(t[:nb])
        t = t[nb:]
    return jnp.concatenate(done, axis=0)


def factor_solve(a, rhs, nblk=64, nb=16):
    n = a.shape[0]
    rr = lax.broadcasted_iota(jnp.int32, (nblk, nblk), 0)
    cc = lax.broadcasted_iota(jnp.int32, (nblk, nblk), 1)
    eye = jnp.where(rr == cc, 1.0, 0.0).astype(F32)
    full = jnp.concatenate([a, rhs], axis=1)
    parts = []
    for p in range(0, n, nblk):
        t = eliminate(jnp.concatenate([full[:nblk, p : p + nblk], eye], axis=1), nblk, nb)
        d = jnp.sum(jnp.where(rr == cc, t[:, :nblk], 0.0), axis=1, keepdims=True)
        inverse = t[:, nblk:] * lax.rsqrt(d)
        top = mm3(inverse, full[:nblk])
        parts.append(top[:, n:])
        if p + nblk < n:
            lower = mm3(full[nblk:, p : p + nblk], inverse, NT)
            full = full[nblk:] - mm3(lower, top)
    return jnp.concatenate(parts, axis=0)


def split_of(level):
    return min(level, CAP)


def kernel(ns, levels, nb_ref, snap_hbm, energy_hbm, sketch_hbm, out, snap, energy, sketch, sketch_t, pad, *scratch):
    (image, gathered, last_modes, joined_energy, joined_image, joined_modes, xp, rs_buf, tm_buf) = scratch[:9]
    (ag_src, ag_buf, gram, coefs, ahead_rows, ahead_coefs, wide_xp, wide_rs, wide_tm, wide_src) = scratch[9:19]
    (wide_ag, wide_gram, in_sem, halo_sem, rs_sem, tm_sem, ag_sem, im_sem, mo_sem, ga_sem) = scratch[19:29]
    (sib_sem, co_sem, ahead_sem, out_sem) = scratch[29:]
    rows = snap.shape[0]
    half = rows // 2
    nblk = rows // K
    piece = K // ns
    scale = 1.0 / (rows * ns)
    t = lax.axis_index("tm")
    s = lax.axis_index("space")
    nt = 2**levels
    core = lax.rem(t, 2)
    halo = HB * K
    pads = pltpu.make_async_copy(snap_hbm, pad.at[pl.ds(halo, rows)], in_sem.at[0])
    loads = [
        pltpu.make_async_copy(snap_hbm, snap, in_sem.at[1]),
        pltpu.make_async_copy(energy_hbm, energy, in_sem.at[2]),
        pltpu.make_async_copy(sketch_hbm, sketch, in_sem.at[3]),
    ]

    ny = min(4, ns)
    nx = ns // ny
    px, py = s // ny, lax.rem(s, ny)
    steps = [(dx, dy) for dx in range(nx) for dy in range(ny) if dx or dy]
    steps.sort(key=lambda step: -min(step[0], nx - step[0]) - min(step[1], ny - step[1]))
    peers = [lax.rem(px + dx, nx) * ny + lax.rem(py + dy, ny) for dx, dy in steps]
    senders = [lax.rem(px + nx - dx, nx) * ny + lax.rem(py + ny - dy, ny) for dx, dy in steps]

    def peer(d):
        return lax.rem(s + d, ns)

    def member(level, d):
        size = 2**level
        return (t // size) * size + lax.rem(lax.rem(t, size) + d, size)

    barrier = pltpu.get_barrier_semaphore()

    def greet_space(d, c):
        pl.semaphore_signal(barrier, inc=1, device_id={"space": peer(d)}, device_id_type=pl.DeviceIdType.MESH)
        return c

    def greet_tm(d, c):
        pl.semaphore_signal(barrier, inc=1, device_id={"tm": lax.rem(t + d, nt)}, device_id_type=pl.DeviceIdType.MESH)
        return c

    lax.fori_loop(1, nt, greet_tm, 0)
    lax.fori_loop(1, ns, greet_space, 0)
    for load in loads:
        load.start()
    pads.start()

    def remote(src, dst, send, recv, where):
        return pltpu.make_async_remote_copy(
            src_ref=src, dst_ref=dst, send_sem=send, recv_sem=recv, device_id=where,
            device_id_type=pl.DeviceIdType.MESH,
        )

    first = s * nblk

    def image_block(b, source, base):
        last = source.shape[0] // K - 1
        places = [jnp.clip(nb_ref[b, k] - base, 0, last) for k in range(energy.shape[1])]
        blocks = [source[pl.ds(place * K, K), :] for place in places]
        left = jnp.concatenate([energy[b, k] for k in range(energy.shape[1])], axis=1)
        acc = 3.0 * snap[b * K : (b + 1) * K, :].astype(F32) + mm(left, jnp.concatenate(blocks, axis=0))
        image[0][b * K : (b + 1) * K, :] = acc.astype(BF16)

    for load in loads:
        load.wait()
    for b in range(HB, nblk - HB):
        image_block(b, snap, first)
    for l in range(levels):
        sketch_t[l] = sketch[l].T
    pads.wait()

    pl.semaphore_wait(barrier, ns - 1 + nt - 1)

    up = remote(snap.at[0:halo], pad.at[halo + rows :], halo_sem.at[0], halo_sem.at[1], {"space": s - 1})
    down = remote(snap.at[rows - halo :], pad.at[0:halo], halo_sem.at[2], halo_sem.at[3], {"space": s + 1})

    @pl.when(s > 0)
    def _():
        up.start()

    @pl.when(s < ns - 1)
    def _():
        down.start()

    @pl.when(s == 0)
    def _():
        pad[0:halo] = jnp.zeros((halo, K), BF16)

    @pl.when(s == ns - 1)
    def _():
        pad[halo + rows :] = jnp.zeros((halo, K), BF16)

    @pl.when(s > 0)
    def _():
        down.wait_recv()

    @pl.when(s < ns - 1)
    def _():
        up.wait_recv()

    for b in (*range(HB), *range(nblk - HB, nblk)):
        image_block(b, pad, first - HB)

    def sum_start(level, partial):
        xp[level] = partial

        for i, q in enumerate(peers):
            remote(
                xp.at[level, pl.ds(q * piece, piece)], rs_buf.at[level, i],
                rs_sem.at[level, 0], rs_sem.at[level, 1], {"space": q},
            ).start()

    def sum_members(level):
        pltpu.make_async_copy(rs_buf.at[level], rs_buf.at[level], rs_sem.at[level, 1]).wait()
        total = xp[level, pl.ds(s * piece, piece), :]
        for i in range(ns - 1):
            total = total + rs_buf[level, i]
        size = 2 ** split_of(level)
        ag_src[level, 0] = total

        def send_member(d, c):
            remote(
                ag_src.at[level, 0], tm_buf[level].at[size - 1 - d],
                tm_sem.at[level, 0], tm_sem.at[level, 1], {"tm": member(split_of(level), d)},
            ).start()
            return c

        lax.fori_loop(1, size, send_member, 0)

    def sum_back(level):
        size = 2 ** split_of(level)
        total = ag_src[level, 0]
        if level:
            pltpu.make_async_copy(tm_buf[level], tm_buf[level], tm_sem.at[level, 1]).wait()
            for i in range(size - 1):
                total = total + tm_buf[level][i]
        total = total * scale
        ag_src[level, 1] = total

        for i, q in enumerate(peers):
            remote(
                ag_src.at[level, 1], ag_buf.at[level, i],
                ag_sem.at[level, 0], ag_sem.at[level, 1], {"space": q},
            ).start()

    def sum_end(level):
        gram[pl.ds(s * piece, piece), :] = ag_src[level, 1]
        pltpu.make_async_copy(ag_buf.at[level], ag_buf.at[level], ag_sem.at[level, 1]).wait()
        for i, q in enumerate(senders):
            gram[pl.ds(q * piece, piece), :] = ag_buf[level, i]
        return gram[...]

    def side_of(level):
        return lax.rem(t // 2 ** (level - 1), 2)

    ahead_side = side_of(AHEAD)
    ahead_partner = {"tm": t + (1 - 2 * ahead_side) * 2 ** (AHEAD - 1)}

    def ahead_exchange(joined):
        keep = rows // 2**AHEAD
        copy = remote(
            joined.at[:, pl.ds((1 - ahead_side) * keep, keep)], ahead_rows.at[ahead_side],
            ahead_sem.at[0], ahead_sem.at[1], ahead_partner,
        )
        copy.start()
        ahead_rows[ahead_side] = joined[:, pl.ds(ahead_side * keep, keep), :]
        sends.append(copy.wait_send)
        return copy

    def wide_start():
        both = [jnp.concatenate([ahead_rows[i, 0], ahead_rows[i, 1]], axis=1) for i in range(2)]
        wide_xp[...] = mm(both[0], both[1], TN).astype(BF16)
        for i, q in enumerate(peers):
            remote(
                wide_xp.at[pl.ds(q * 2 * piece, 2 * piece)], wide_rs.at[i],
                ahead_sem.at[2], ahead_sem.at[3], {"space": q},
            ).start()

    def wide_members():
        pltpu.make_async_copy(wide_rs, wide_rs, ahead_sem.at[3]).wait()
        total = wide_xp[pl.ds(s * 2 * piece, 2 * piece), :].astype(F32)
        for i in range(ns - 1):
            total = total + wide_rs[i].astype(F32)
        wide_src[0] = total.astype(BF16)
        size = 2**AHEAD

        def send_member(d, c):
            remote(
                wide_src.at[0], wide_tm.at[size - 1 - d],
                ahead_sem.at[4], ahead_sem.at[5], {"tm": member(AHEAD, d)},
            ).start()
            return c

        lax.fori_loop(1, size, send_member, 0)

    def wide_back():
        pltpu.make_async_copy(wide_tm, wide_tm, ahead_sem.at[5]).wait()
        total = wide_src[0].astype(F32)
        for i in range(2**AHEAD - 1):
            total = total + wide_tm[i].astype(F32)
        wide_src[1] = (total * scale).astype(BF16)
        for i, q in enumerate(peers):
            remote(wide_src.at[1], wide_ag.at[i], ahead_sem.at[6], ahead_sem.at[7], {"space": q}).start()

    def wide_end():
        wide_gram[pl.ds(s * 2 * piece, 2 * piece), :] = wide_src[1]
        pltpu.make_async_copy(wide_ag, wide_ag, ahead_sem.at[7]).wait()
        for i, q in enumerate(senders):
            wide_gram[pl.ds(q * 2 * piece, 2 * piece), :] = wide_ag[i]
        return wide_gram[...].astype(F32)

    def ahead_coefs_exchange(coef):
        ahead_coefs[ahead_side] = coef
        copy = remote(
            ahead_coefs.at[ahead_side], ahead_coefs.at[ahead_side], ahead_sem.at[8], ahead_sem.at[9], ahead_partner
        )
        copy.start()
        sends.append(copy.wait_send)
        return copy

    sends = []

    def exchange(level, source, start, joined, sem):
        side = side_of(level)
        keep = rows // 2 ** split_of(level)
        other, own = ((1 - side) * keep, side * keep) if level <= CAP else (0, 0)
        copy = remote(
            source.at[pl.ds(start + other, keep)], joined.at[side],
            sem.at[level, 0], sem.at[level, 1], {"tm": t + (1 - 2 * side) * 2 ** (level - 1)},
        )
        copy.start()
        joined[side] = source[pl.ds(start + own, keep), :]
        sends.append(copy.wait_send)
        return copy

    def slot_of(level):
        return side_of(levels) if level == levels - 1 else 0

    def mine(level, start):
        return gathered[level].at[:, pl.ds(start, rows // 2 ** split_of(level))]

    def gather(level, start):
        size = 2 ** split_of(level)

        def send_modes(d, c):
            remote(
                mine(level, start), mine(level, start), ga_sem.at[level, 0], ga_sem.at[level, 1],
                {"tm": member(split_of(level), 2 * d)},
            ).start()
            return c

        lax.fori_loop(1, size // 2, send_modes, 0)

    def gather_bytes(level, i):
        count = rows // 2 ** split_of(level)
        some = gathered[level].at[:, 0 : (2 ** split_of(level) // 2 - 1) * count]
        return pltpu.make_async_copy(some, some, ga_sem.at[level, i])

    def to_sibling(level):
        if split_of(level) > 1:
            gather_bytes(level, 1).wait()
            sends.append(gather_bytes(level, 0).wait)
        whole = gathered[level].at[:, pl.ds(core * half, half)]
        copy = remote(whole, whole, sib_sem.at[level, 0], sib_sem.at[level, 1], {"tm": t + 1 - 2 * core})
        copy.start()
        sends.append(copy.wait_send)
        return copy

    def store(level):
        copy = pltpu.make_async_copy(gathered[level].at[slot_of(level)], out.at[level, 0], out_sem.at[level])
        copy.start()
        sends.append(copy.wait)

    rr = lax.broadcasted_iota(jnp.int32, (K, K), 0)
    cc = lax.broadcasted_iota(jnp.int32, (K, K), 1)
    eye = jnp.where(rr == cc, 1.0, 0.0).astype(F32)
    energy_copy = exchange(1, image[0], 0, joined_energy, im_sem)
    sum_start(0, mm(image[0][...], image[0][...], TN))
    energy_copy.wait_recv()
    sum_start(1, mm(joined_energy[0], joined_energy[1], TN))
    sum_members(0)
    sum_back(0)
    sum_members(1)
    sum_back(1)
    coef = factor_solve(sum_end(0), eye).astype(BF16)
    coefs[core] = coef
    coefs_copy = remote(coefs.at[core], coefs.at[core], co_sem.at[0], co_sem.at[1], {"tm": t + 1 - 2 * core})
    coefs_copy.start()
    sends.append(coefs_copy.wait_send)
    gathered[0][0] = mm(snap[...], coef, NT).astype(BF16)
    modes_copy = exchange(1, gathered[0].at[0], 0, joined_modes[0], mo_sem)
    store(0)

    offset = 0 * t
    siblings = {}
    for level in range(1, levels + 1):
        ji = joined_image[level - 1]
        jm = joined_modes[level - 1]
        if level == 1:
            coefs_copy.wait_recv()
            for i in range(2):
                ji[i] = mm(joined_energy[i], coefs[i], NT).astype(BF16)
            x = mm2(mm2(sum_end(1), coefs[1], NT).T, coefs[0], NT).T
        elif level == AHEAD:
            if level < levels:
                gather(level - 1, offset)
            siblings[level - 2].wait_recv()
            store(level - 2)
            coefs_copy.wait_recv()
            for i in range(2):
                left, right = ahead_coefs[i, :, :K], ahead_coefs[i, :, K:]
                ji[i] = (mm(ahead_rows[i, 0], left, NT) + mm(ahead_rows[i, 1], right, NT)).astype(BF16)
            x = around(ahead_coefs[0], wide_end(), ahead_coefs[1])
            if level == levels:
                modes_copy.wait_recv()
                gather(level - 1, offset)
            siblings[level - 1] = to_sibling(level - 1)
        else:
            image_copy.wait_recv()
            sum_start(level, mm(ji[0], ji[1], TN))
            if level == AHEAD - 1:
                rows_copy = ahead_exchange(ji)
            if level - 1 >= 1 and level < levels and split_of(level - 1) > 1:
                gather(level - 1, offset)
            if level - 2 >= 1:
                siblings[level - 2].wait_recv()
                store(level - 2)
            sum_members(level)
            if level == levels:
                modes_copy.wait_recv()
                if split_of(level - 1) > 1:
                    gather(level - 1, offset)
            sum_back(level)
            if level == AHEAD - 1:
                rows_copy.wait_recv()
                wide_start()
            x = sum_end(level)
            siblings[level - 1] = to_sibling(level - 1)
        st = sketch_t[level - 1]
        st0, st1 = st[:, :K], st[:, K:]
        y0 = st0 + mm3(st1, x, NT)
        y1 = st1 + mm3(st0, x)
        z0 = y0 + mm3(y1, x, NT)
        z1 = y1 + mm3(y0, x)
        y = jnp.concatenate([y0, y1], axis=1)
        z = jnp.concatenate([z0, z1], axis=1)
        inner = mm3(y, z, NT)
        if level == AHEAD - 1:
            wide_members()
        coef = factor_solve(inner, y).astype(BF16)
        if level == AHEAD - 1:
            coefs_copy = ahead_coefs_exchange(coef)
            wide_back()
        c0, c1 = coef[:, :K], coef[:, K:]
        keep = rows // 2 ** split_of(level)
        if level <= CAP:
            offset = offset + side_of(level) * keep
        if level < levels:
            if level != AHEAD - 1:
                image[level][...] = (mm(ji[0], c0, NT) + mm(ji[1], c1, NT)).astype(BF16)
                image_copy = exchange(level + 1, image[level], 0, joined_image[level], im_sem)
            modes_copy.wait_recv()
            target = gathered[level].at[slot_of(level)]
            target[pl.ds(offset, keep), :] = (mm(jm[0], c0, NT) + mm(jm[1], c1, NT)).astype(BF16)
            if level < levels - 1:
                modes_copy = exchange(level + 1, target, offset, joined_modes[level], mo_sem)
            else:
                side = side_of(levels)
                chunk = target.at[pl.ds(offset, keep)]
                modes_copy = remote(
                    chunk, chunk, mo_sem.at[levels, 0], mo_sem.at[levels, 1],
                    {"tm": t + (1 - 2 * side) * 2 ** (levels - 1)},
                )
                modes_copy.start()
                sends.append(modes_copy.wait_send)
        else:
            siblings[level - 1].wait_recv()
            store(level - 1)
            pair = gathered[level - 1]
            for i in range(4):
                part = slice(i * rows // 4, (i + 1) * rows // 4)
                last_modes[part] = (mm(pair[0, part], c0, NT) + mm(pair[1, part], c1, NT)).astype(BF16)
                copy = pltpu.make_async_copy(last_modes.at[part], out.at[level, 0, part], out_sem.at[level + i])
                copy.start()
                sends.append(copy.wait)

    @pl.when(s > 0)
    def _():
        up.wait_send()

    @pl.when(s < ns - 1)
    def _():
        down.wait_send()

    pltpu.make_async_copy(wide_rs, wide_rs, ahead_sem.at[2]).wait()
    pltpu.make_async_copy(wide_tm, wide_tm, ahead_sem.at[4]).wait()
    pltpu.make_async_copy(wide_ag, wide_ag, ahead_sem.at[6]).wait()
    for level in range(levels + 1):
        if level == AHEAD:
            continue
        pltpu.make_async_copy(rs_buf.at[level], rs_buf.at[level], rs_sem.at[level, 0]).wait()
        if level:
            pltpu.make_async_copy(tm_buf[level], tm_buf[level], tm_sem.at[level, 0]).wait()
        pltpu.make_async_copy(ag_buf.at[level], ag_buf.at[level], ag_sem.at[level, 0]).wait()
    for wait in sends:
        wait()


def on_device(ns, levels, snapshots, energy, neighbours, sketch):
    rows = snapshots.shape[0]
    half = rows // 2
    count = levels + 1
    piece = K // ns
    sems = lambda *shape: pltpu.SemaphoreType.DMA(shape)
    hbm = pl.BlockSpec(memory_space=pltpu.HBM)
    return pl.pallas_call(
        functools.partial(kernel, ns, levels),
        out_shape=jax.ShapeDtypeStruct((count, 1, rows, K), BF16),
        in_specs=[pl.BlockSpec(memory_space=pltpu.SMEM), hbm, hbm, hbm],
        out_specs=hbm,
        scratch_shapes=[
            pltpu.VMEM(snapshots.shape, BF16),
            pltpu.VMEM(energy.shape, BF16),
            pltpu.VMEM(sketch.shape, F32),
            pltpu.VMEM((levels, K, 2 * K), F32),
            pltpu.VMEM((rows + 2 * HB * K, K), BF16),
            [pltpu.VMEM((rows // 2 ** split_of(l), K), BF16) for l in range(levels)],
            [pltpu.VMEM((2 if l == levels - 1 else 1, rows, K), BF16) for l in range(levels)],
            pltpu.VMEM((rows, K), BF16),
            pltpu.VMEM((2, half, K), BF16),
            [pltpu.VMEM((2, rows // 2 ** split_of(l), K), BF16) for l in range(1, count)],
            [pltpu.VMEM((2, rows // 2 ** split_of(l), K), BF16) for l in range(1, count)],
            pltpu.VMEM((count, K, K), F32),
            pltpu.VMEM((count, ns - 1, piece, K), F32),
            [pltpu.VMEM((max(2 ** split_of(l) - 1, 1), piece, K), F32) for l in range(count)],
            pltpu.VMEM((count, 2, piece, K), F32),
            pltpu.VMEM((count, ns - 1, piece, K), F32),
            pltpu.VMEM((K, K), F32),
            pltpu.VMEM((2, K, K), BF16),
            pltpu.VMEM((2, 2, rows // 2**AHEAD, K), BF16),
            pltpu.VMEM((2, K, 2 * K), BF16),
            pltpu.VMEM((2 * K, 2 * K), BF16),
            pltpu.VMEM((ns - 1, 2 * piece, 2 * K), BF16),
            pltpu.VMEM((2**AHEAD - 1, 2 * piece, 2 * K), BF16),
            pltpu.VMEM((2, 2 * piece, 2 * K), BF16),
            pltpu.VMEM((ns - 1, 2 * piece, 2 * K), BF16),
            pltpu.VMEM((2 * K, 2 * K), BF16),
            sems(4),
            sems(4),
            *[sems(count, 2)] * 7,
            sems(2),
            sems(10),
            sems(count + 4),
        ],
        compiler_params=pltpu.CompilerParams(
            collective_id=0, has_side_effects=True, vmem_limit_bytes=40 * 1024 * 1024
        ),
    )(neighbours, snapshots, energy, sketch)


def solution(mesh):
    placed = (P("space", "tm"), P("space", None, None, None), P("space", None), P())
    ns = mesh.shape["space"]
    levels = mesh.shape["tm"].bit_length() - 1
    return jax.shard_map(
        functools.partial(on_device, ns, levels),
        mesh=mesh,
        in_specs=placed,
        out_specs=P(None, "tm", "space", None),
        check_vma=False,
    )
```

```python
import functools

import jax
import jax.numpy as jnp
from jax import lax
from jax.experimental import pallas as pl
from jax.experimental.pallas import tpu as pltpu
from jax.sharding import PartitionSpec as P

K = 128
HB = 2
CAP = 3
AHEAD = 3
F32 = jnp.float32
BF16 = jnp.bfloat16
NN = ((1,), (0,))
NT = ((1,), (1,))
TN = ((0,), (0,))


def mm(a, b, dims=NN):
    return lax.dot_general(a, b, (dims, ((), ())), preferred_element_type=F32)


def split(a):
    high = a.astype(BF16)
    return high, (a - high.astype(F32)).astype(BF16)


def mm3(a, b, dims=NN):
    ah, al = split(a)
    bh, bl = split(b)
    return mm(ah, bh, dims) + (mm(ah, bl, dims) + mm(al, bh, dims))


def mm2(a, b, dims=NN):
    ah, al = split(a)
    return mm(ah, b, dims) + mm(al, b, dims)


def around(a, middle, b):
    high, low = split(mm2(middle, b, NT))
    return mm(a, high) + mm(a, low)


def eliminate(t, n, nb):
    done = []
    for k0 in range(0, n, nb):
        rows = lax.broadcasted_iota(jnp.int32, t.shape, 0)
        cols = [jnp.broadcast_to(t[:, k0 + j : k0 + j + 1], t.shape) for j in range(nb)]
        for j in range(nb):
            pivot = 1.0 / cols[j][j : j + 1, :]
            factor = jnp.where(rows > j, cols[j] * pivot, 0.0)
            for i in range(j + 1, nb):
                cols[i] = cols[i] - factor * cols[i][j : j + 1, :]
            t = t - factor * t[j : j + 1, :]
        done.append(t[:nb])
        t = t[nb:]
    return jnp.concatenate(done, axis=0)


def factor_solve(a, rhs, nblk=64, nb=16):
    n = a.shape[0]
    rr = lax.broadcasted_iota(jnp.int32, (nblk, nblk), 0)
    cc = lax.broadcasted_iota(jnp.int32, (nblk, nblk), 1)
    eye = jnp.where(rr == cc, 1.0, 0.0).astype(F32)
    full = jnp.concatenate([a, rhs], axis=1)
    parts = []
    for p in range(0, n, nblk):
        t = eliminate(jnp.concatenate([full[:nblk, p : p + nblk], eye], axis=1), nblk, nb)
        d = jnp.sum(jnp.where(rr == cc, t[:, :nblk], 0.0), axis=1, keepdims=True)
        inverse = t[:, nblk:] * lax.rsqrt(d)
        top = mm3(inverse, full[:nblk])
        parts.append(top[:, n:])
        if p + nblk < n:
            lower = mm3(full[nblk:, p : p + nblk], inverse, NT)
            full = full[nblk:] - mm3(lower, top)
    return jnp.concatenate(parts, axis=0)


def split_of(level):
    return min(level, CAP)


def kernel(ns, levels, nb_ref, snap_hbm, energy_hbm, sketch_hbm, out, snap, energy, sketch, sketch_t, pad, *scratch):
    (image, gathered, last_modes, joined_energy, joined_image, joined_modes, xp, rs_buf, tm_buf) = scratch[:9]
    (ag_src, ag_buf, gram, coefs, ahead_rows, ahead_coefs, wide_xp, wide_rs, wide_tm, wide_src) = scratch[9:19]
    (wide_ag, wide_gram, in_sem, halo_sem, rs_sem, tm_sem, ag_sem, im_sem, mo_sem, ga_sem) = scratch[19:29]
    (sib_sem, co_sem, ahead_sem, out_sem) = scratch[29:]
    rows = snap.shape[0]
    half = rows // 2
    nblk = rows // K
    piece = K // ns
    scale = 1.0 / (rows * ns)
    t = lax.axis_index("tm")
    s = lax.axis_index("space")
    nt = 2**levels
    core = lax.rem(t, 2)
    halo = HB * K
    pads = pltpu.make_async_copy(snap_hbm, pad.at[pl.ds(halo, rows)], in_sem.at[0])
    loads = [
        pltpu.make_async_copy(snap_hbm, snap, in_sem.at[1]),
        pltpu.make_async_copy(energy_hbm, energy, in_sem.at[2]),
        pltpu.make_async_copy(sketch_hbm, sketch, in_sem.at[3]),
    ]

    ny = min(4, ns)
    nx = ns // ny
    px, py = s // ny, lax.rem(s, ny)
    steps = [(dx, dy) for dx in range(nx) for dy in range(ny) if dx or dy]
    steps.sort(key=lambda step: -min(step[0], nx - step[0]) - min(step[1], ny - step[1]))
    peers = [lax.rem(px + dx, nx) * ny + lax.rem(py + dy, ny) for dx, dy in steps]
    senders = [lax.rem(px + nx - dx, nx) * ny + lax.rem(py + ny - dy, ny) for dx, dy in steps]

    def peer(d):
        return lax.rem(s + d, ns)

    def member(level, d):
        size = 2**level
        return (t // size) * size + lax.rem(lax.rem(t, size) + d, size)

    barrier = pltpu.get_barrier_semaphore()

    def greet_space(d, c):
        pl.semaphore_signal(barrier, inc=1, device_id={"space": peer(d)}, device_id_type=pl.DeviceIdType.MESH)
        return c

    def greet_tm(d, c):
        pl.semaphore_signal(barrier, inc=1, device_id={"tm": lax.rem(t + d, nt)}, device_id_type=pl.DeviceIdType.MESH)
        return c

    lax.fori_loop(1, nt, greet_tm, 0)
    lax.fori_loop(1, ns, greet_space, 0)
    for load in loads:
        load.start()
    pads.start()

    def remote(src, dst, send, recv, where):
        return pltpu.make_async_remote_copy(
            src_ref=src, dst_ref=dst, send_sem=send, recv_sem=recv, device_id=where,
            device_id_type=pl.DeviceIdType.MESH,
        )

    first = s * nblk

    def image_block(b, source, base):
        last = source.shape[0] // K - 1
        places = [jnp.clip(nb_ref[b, k] - base, 0, last) for k in range(energy.shape[1])]
        blocks = [source[pl.ds(place * K, K), :] for place in places]
        left = jnp.concatenate([energy[b, k] for k in range(energy.shape[1])], axis=1)
        acc = 3.0 * snap[b * K : (b + 1) * K, :].astype(F32) + mm(left, jnp.concatenate(blocks, axis=0))
        image[0][b * K : (b + 1) * K, :] = acc.astype(BF16)

    for load in loads:
        load.wait()
    for b in range(HB, nblk - HB):
        image_block(b, snap, first)
    for l in range(levels):
        sketch_t[l] = sketch[l].T
    pads.wait()

    pl.semaphore_wait(barrier, ns - 1 + nt - 1)

    up = remote(snap.at[0:halo], pad.at[halo + rows :], halo_sem.at[0], halo_sem.at[1], {"space": s - 1})
    down = remote(snap.at[rows - halo :], pad.at[0:halo], halo_sem.at[2], halo_sem.at[3], {"space": s + 1})

    @pl.when(s > 0)
    def _():
        up.start()

    @pl.when(s < ns - 1)
    def _():
        down.start()

    @pl.when(s == 0)
    def _():
        pad[0:halo] = jnp.zeros((halo, K), BF16)

    @pl.when(s == ns - 1)
    def _():
        pad[halo + rows :] = jnp.zeros((halo, K), BF16)

    @pl.when(s > 0)
    def _():
        down.wait_recv()

    @pl.when(s < ns - 1)
    def _():
        up.wait_recv()

    for b in (*range(HB), *range(nblk - HB, nblk)):
        image_block(b, pad, first - HB)

    def sum_start(level, partial):
        xp[level] = partial

        for i, q in enumerate(peers):
            remote(
                xp.at[level, pl.ds(q * piece, piece)], rs_buf.at[level, i],
                rs_sem.at[level, 0], rs_sem.at[level, 1], {"space": q},
            ).start()

    def sum_members(level):
        pltpu.make_async_copy(rs_buf.at[level], rs_buf.at[level], rs_sem.at[level, 1]).wait()
        total = xp[level, pl.ds(s * piece, piece), :]
        for i in range(ns - 1):
            total = total + rs_buf[level, i]
        size = 2 ** split_of(level)
        ag_src[level, 0] = total

        def send_member(d, c):
            remote(
                ag_src.at[level, 0], tm_buf[level].at[size - 1 - d],
                tm_sem.at[level, 0], tm_sem.at[level, 1], {"tm": member(split_of(level), d)},
            ).start()
            return c

        lax.fori_loop(1, size, send_member, 0)

    def sum_back(level):
        size = 2 ** split_of(level)
        total = ag_src[level, 0]
        if level:
            pltpu.make_async_copy(tm_buf[level], tm_buf[level], tm_sem.at[level, 1]).wait()
            for i in range(size - 1):
                total = total + tm_buf[level][i]
        total = total * scale
        ag_src[level, 1] = total

        for i, q in enumerate(peers):
            remote(
                ag_src.at[level, 1], ag_buf.at[level, i],
                ag_sem.at[level, 0], ag_sem.at[level, 1], {"space": q},
            ).start()

    def sum_end(level):
        gram[pl.ds(s * piece, piece), :] = ag_src[level, 1]
        pltpu.make_async_copy(ag_buf.at[level], ag_buf.at[level], ag_sem.at[level, 1]).wait()
        for i, q in enumerate(senders):
            gram[pl.ds(q * piece, piece), :] = ag_buf[level, i]
        return gram[...]

    def side_of(level):
        return lax.rem(t // 2 ** (level - 1), 2)

    ahead_side = side_of(AHEAD)
    ahead_partner = {"tm": t + (1 - 2 * ahead_side) * 2 ** (AHEAD - 1)}

    def ahead_exchange(joined):
        keep = rows // 2**AHEAD
        copy = remote(
            joined.at[:, pl.ds((1 - ahead_side) * keep, keep)], ahead_rows.at[ahead_side],
            ahead_sem.at[0], ahead_sem.at[1], ahead_partner,
        )
        copy.start()
        ahead_rows[ahead_side] = joined[:, pl.ds(ahead_side * keep, keep), :]
        sends.append(copy.wait_send)
        return copy

    def wide_start():
        both = [jnp.concatenate([ahead_rows[i, 0], ahead_rows[i, 1]], axis=1) for i in range(2)]
        wide_xp[...] = mm(both[0], both[1], TN).astype(BF16)
        for i, q in enumerate(peers):
            remote(
                wide_xp.at[pl.ds(q * 2 * piece, 2 * piece)], wide_rs.at[i],
                ahead_sem.at[2], ahead_sem.at[3], {"space": q},
            ).start()

    def wide_members():
        pltpu.make_async_copy(wide_rs, wide_rs, ahead_sem.at[3]).wait()
        total = wide_xp[pl.ds(s * 2 * piece, 2 * piece), :].astype(F32)
        for i in range(ns - 1):
            total = total + wide_rs[i].astype(F32)
        wide_src[0] = total.astype(BF16)
        size = 2**AHEAD

        def send_member(d, c):
            remote(
                wide_src.at[0], wide_tm.at[size - 1 - d],
                ahead_sem.at[4], ahead_sem.at[5], {"tm": member(AHEAD, d)},
            ).start()
            return c

        lax.fori_loop(1, size, send_member, 0)

    def wide_back():
        pltpu.make_async_copy(wide_tm, wide_tm, ahead_sem.at[5]).wait()
        total = wide_src[0].astype(F32)
        for i in range(2**AHEAD - 1):
            total = total + wide_tm[i].astype(F32)
        wide_src[1] = (total * scale).astype(BF16)
        for i, q in enumerate(peers):
            remote(wide_src.at[1], wide_ag.at[i], ahead_sem.at[6], ahead_sem.at[7], {"space": q}).start()

    def wide_end():
        wide_gram[pl.ds(s * 2 * piece, 2 * piece), :] = wide_src[1]
        pltpu.make_async_copy(wide_ag, wide_ag, ahead_sem.at[7]).wait()
        for i, q in enumerate(senders):
            wide_gram[pl.ds(q * 2 * piece, 2 * piece), :] = wide_ag[i]
        return wide_gram[...].astype(F32)

    def ahead_coefs_exchange(coef):
        ahead_coefs[ahead_side] = coef
        copy = remote(
            ahead_coefs.at[ahead_side], ahead_coefs.at[ahead_side], ahead_sem.at[8], ahead_sem.at[9], ahead_partner
        )
        copy.start()
        sends.append(copy.wait_send)
        return copy

    sends = []

    def exchange(level, source, start, joined, sem):
        side = side_of(level)
        keep = rows // 2 ** split_of(level)
        other, own = ((1 - side) * keep, side * keep) if level <= CAP else (0, 0)
        copy = remote(
            source.at[pl.ds(start + other, keep)], joined.at[side],
            sem.at[level, 0], sem.at[level, 1], {"tm": t + (1 - 2 * side) * 2 ** (level - 1)},
        )
        copy.start()
        joined[side] = source[pl.ds(start + own, keep), :]
        sends.append(copy.wait_send)
        return copy

    def slot_of(level):
        return side_of(levels) if level == levels - 1 else 0

    def mine(level, start):
        return gathered[level].at[:, pl.ds(start, rows // 2 ** split_of(level))]

    def gather(level, start):
        size = 2 ** split_of(level)

        def send_modes(d, c):
            remote(
                mine(level, start), mine(level, start), ga_sem.at[level, 0], ga_sem.at[level, 1],
                {"tm": member(split_of(level), 2 * d)},
            ).start()
            return c

        lax.fori_loop(1, size // 2, send_modes, 0)

    def gather_bytes(level, i):
        count = rows // 2 ** split_of(level)
        some = gathered[level].at[:, 0 : (2 ** split_of(level) // 2 - 1) * count]
        return pltpu.make_async_copy(some, some, ga_sem.at[level, i])

    def to_sibling(level):
        if split_of(level) > 1:
            gather_bytes(level, 1).wait()
            sends.append(gather_bytes(level, 0).wait)
        whole = gathered[level].at[:, pl.ds(core * half, half)]
        copy = remote(whole, whole, sib_sem.at[level, 0], sib_sem.at[level, 1], {"tm": t + 1 - 2 * core})
        copy.start()
        sends.append(copy.wait_send)
        return copy

    def store(level):
        copy = pltpu.make_async_copy(gathered[level].at[slot_of(level)], out.at[level, 0], out_sem.at[level])
        copy.start()
        sends.append(copy.wait)

    rr = lax.broadcasted_iota(jnp.int32, (K, K), 0)
    cc = lax.broadcasted_iota(jnp.int32, (K, K), 1)
    eye = jnp.where(rr == cc, 1.0, 0.0).astype(F32)
    energy_copy = exchange(1, image[0], 0, joined_energy, im_sem)
    sum_start(0, mm(image[0][...], image[0][...], TN))
    energy_copy.wait_recv()
    sum_start(1, mm(joined_energy[0], joined_energy[1], TN))
    sum_members(0)
    sum_back(0)
    sum_members(1)
    sum_back(1)
    coef = factor_solve(sum_end(0), eye).astype(BF16)
    coefs[core] = coef
    coefs_copy = remote(coefs.at[core], coefs.at[core], co_sem.at[0], co_sem.at[1], {"tm": t + 1 - 2 * core})
    coefs_copy.start()
    sends.append(coefs_copy.wait_send)
    gathered[0][0] = mm(snap[...], coef, NT).astype(BF16)
    modes_copy = exchange(1, gathered[0].at[0], 0, joined_modes[0], mo_sem)
    store(0)

    offset = 0 * t
    siblings = {}
    for level in range(1, levels + 1):
        ji = joined_image[level - 1]
        jm = joined_modes[level - 1]
        if level == 1:
            coefs_copy.wait_recv()
            for i in range(2):
                ji[i] = mm(joined_energy[i], coefs[i], NT).astype(BF16)
            x = mm2(mm2(sum_end(1), coefs[1], NT).T, coefs[0], NT).T
        elif level == AHEAD:
            if level < levels:
                gather(level - 1, offset)
            siblings[level - 2].wait_recv()
            store(level - 2)
            coefs_copy.wait_recv()
            for i in range(2):
                left, right = ahead_coefs[i, :, :K], ahead_coefs[i, :, K:]
                ji[i] = (mm(ahead_rows[i, 0], left, NT) + mm(ahead_rows[i, 1], right, NT)).astype(BF16)
            x = around(ahead_coefs[0], wide_end(), ahead_coefs[1])
            if level == levels:
                modes_copy.wait_recv()
                gather(level - 1, offset)
            siblings[level - 1] = to_sibling(level - 1)
        else:
            image_copy.wait_recv()
            sum_start(level, mm(ji[0], ji[1], TN))
            if level == AHEAD - 1:
                rows_copy = ahead_exchange(ji)
            modes_copy = start_modes()
            if level - 1 >= 1 and level < levels and split_of(level - 1) > 1:
                gather(level - 1, offset)
            if level - 2 >= 1:
                siblings[level - 2].wait_recv()
                store(level - 2)
            sum_members(level)
            sum_back(level)
            if level == levels:
                modes_copy.wait_recv()
                if split_of(level - 1) > 1:
                    gather(level - 1, offset)
            if level == AHEAD - 1:
                rows_copy.wait_recv()
                wide_start()
            x = sum_end(level)
            if level < levels:
                siblings[level - 1] = to_sibling(level - 1)
        st = sketch_t[level - 1]
        st0, st1 = st[:, :K], st[:, K:]
        y0 = st0 + mm3(st1, x, NT)
        y1 = st1 + mm3(st0, x)
        z0 = y0 + mm3(y1, x, NT)
        z1 = y1 + mm3(y0, x)
        y = jnp.concatenate([y0, y1], axis=1)
        z = jnp.concatenate([z0, z1], axis=1)
        inner = mm3(y, z, NT)
        if level == AHEAD - 1:
            wide_members()
        coef = factor_solve(inner, y).astype(BF16)
        if level == AHEAD - 1:
            coefs_copy = ahead_coefs_exchange(coef)
            wide_back()
        c0, c1 = coef[:, :K], coef[:, K:]
        keep = rows // 2 ** split_of(level)
        if level <= CAP:
            offset = offset + side_of(level) * keep
        if level < levels:
            if level != AHEAD - 1:
                image[level][...] = (mm(ji[0], c0, NT) + mm(ji[1], c1, NT)).astype(BF16)
                image_copy = exchange(level + 1, image[level], 0, joined_image[level], im_sem)
            modes_copy.wait_recv()
            target = gathered[level].at[slot_of(level)]
            target[pl.ds(offset, keep), :] = (mm(jm[0], c0, NT) + mm(jm[1], c1, NT)).astype(BF16)

            def start_modes(level=level, target=target, start=offset, keep=keep):
                if level < levels - 1:
                    return exchange(level + 1, target, start, joined_modes[level], mo_sem)
                side = side_of(levels)
                chunk = target.at[pl.ds(start, keep)]
                copy = remote(
                    chunk, chunk, mo_sem.at[levels, 0], mo_sem.at[levels, 1],
                    {"tm": t + (1 - 2 * side) * 2 ** (levels - 1)},
                )
                copy.start()
                sends.append(copy.wait_send)
                return copy

            if level + 1 == AHEAD:
                modes_copy = start_modes()
        else:
            if level != AHEAD:
                siblings[level - 1] = to_sibling(level - 1)
            pair = gathered[level - 1]
            for i in range(4):
                if i == 2:
                    siblings[level - 1].wait_recv()
                    store(level - 1)
                part = pl.ds((core if i < 2 else 1 - core) * half + i % 2 * (half // 2), half // 2)
                last_modes[part] = (mm(pair[0, part], c0, NT) + mm(pair[1, part], c1, NT)).astype(BF16)
                copy = pltpu.make_async_copy(last_modes.at[part], out.at[level, 0, part], out_sem.at[level + i])
                copy.start()
                sends.append(copy.wait)

    @pl.when(s > 0)
    def _():
        up.wait_send()

    @pl.when(s < ns - 1)
    def _():
        down.wait_send()

    pltpu.make_async_copy(wide_rs, wide_rs, ahead_sem.at[2]).wait()
    pltpu.make_async_copy(wide_tm, wide_tm, ahead_sem.at[4]).wait()
    pltpu.make_async_copy(wide_ag, wide_ag, ahead_sem.at[6]).wait()
    for level in range(levels + 1):
        if level == AHEAD:
            continue
        pltpu.make_async_copy(rs_buf.at[level], rs_buf.at[level], rs_sem.at[level, 0]).wait()
        if level:
            pltpu.make_async_copy(tm_buf[level], tm_buf[level], tm_sem.at[level, 0]).wait()
        pltpu.make_async_copy(ag_buf.at[level], ag_buf.at[level], ag_sem.at[level, 0]).wait()
    for wait in sends:
        wait()


def on_device(ns, levels, snapshots, energy, neighbours, sketch):
    rows = snapshots.shape[0]
    half = rows // 2
    count = levels + 1
    piece = K // ns
    sems = lambda *shape: pltpu.SemaphoreType.DMA(shape)
    hbm = pl.BlockSpec(memory_space=pltpu.HBM)
    return pl.pallas_call(
        functools.partial(kernel, ns, levels),
        out_shape=jax.ShapeDtypeStruct((count, 1, rows, K), BF16),
        in_specs=[pl.BlockSpec(memory_space=pltpu.SMEM), hbm, hbm, hbm],
        out_specs=hbm,
        scratch_shapes=[
            pltpu.VMEM(snapshots.shape, BF16),
            pltpu.VMEM(energy.shape, BF16),
            pltpu.VMEM(sketch.shape, F32),
            pltpu.VMEM((levels, K, 2 * K), F32),
            pltpu.VMEM((rows + 2 * HB * K, K), BF16),
            [pltpu.VMEM((rows // 2 ** split_of(l), K), BF16) for l in range(levels)],
            [pltpu.VMEM((2 if l == levels - 1 else 1, rows, K), BF16) for l in range(levels)],
            pltpu.VMEM((rows, K), BF16),
            pltpu.VMEM((2, half, K), BF16),
            [pltpu.VMEM((2, rows // 2 ** split_of(l), K), BF16) for l in range(1, count)],
            [pltpu.VMEM((2, rows // 2 ** split_of(l), K), BF16) for l in range(1, count)],
            pltpu.VMEM((count, K, K), F32),
            pltpu.VMEM((count, ns - 1, piece, K), F32),
            [pltpu.VMEM((max(2 ** split_of(l) - 1, 1), piece, K), F32) for l in range(count)],
            pltpu.VMEM((count, 2, piece, K), F32),
            pltpu.VMEM((count, ns - 1, piece, K), F32),
            pltpu.VMEM((K, K), F32),
            pltpu.VMEM((2, K, K), BF16),
            pltpu.VMEM((2, 2, rows // 2**AHEAD, K), BF16),
            pltpu.VMEM((2, K, 2 * K), BF16),
            pltpu.VMEM((2 * K, 2 * K), BF16),
            pltpu.VMEM((ns - 1, 2 * piece, 2 * K), BF16),
            pltpu.VMEM((2**AHEAD - 1, 2 * piece, 2 * K), BF16),
            pltpu.VMEM((2, 2 * piece, 2 * K), BF16),
            pltpu.VMEM((ns - 1, 2 * piece, 2 * K), BF16),
            pltpu.VMEM((2 * K, 2 * K), BF16),
            sems(4),
            sems(4),
            *[sems(count, 2)] * 7,
            sems(2),
            sems(10),
            sems(count + 4),
        ],
        compiler_params=pltpu.CompilerParams(
            collective_id=0, has_side_effects=True, vmem_limit_bytes=40 * 1024 * 1024
        ),
    )(neighbours, snapshots, energy, sketch)


def solution(mesh):
    placed = (P("space", "tm"), P("space", None, None, None), P("space", None), P())
    ns = mesh.shape["space"]
    levels = mesh.shape["tm"].bit_length() - 1
    return jax.shard_map(
        functools.partial(on_device, ns, levels),
        mesh=mesh,
        in_specs=placed,
        out_specs=P(None, "tm", "space", None),
        check_vma=False,
    )
```
